32 devices in a mesh: groups: 2 (over y), aux: 4 (over z), atoms: 4 (over x, core).
Axes of the slice: x: 2, y: 2, z: 4, core: 2. Of those that a mesh axis runs over, the one named last changes fastest.
Arguments:
- three_center: bfloat16 [2048, 4, 3, 128], P('atoms', 'aux'), may hold values from -0.3125 to 0.3125
- virt_density: bfloat16 [4096, 2048], P(('groups', 'atoms')), parts along dimension 0, may hold values from -6 to 6
- occ_density: bfloat16 [4096, 2048], P('groups', 'atoms'), parts along dimension 0, as said below
- partner_list: int32 [16, 3], replicated, may hold values from 0 to 15, as said below
- partner_count: int32 [16], replicated, may hold values from 1 to 3, 30 in all
Outputs:
- polarizability: float32 [8, 4], P(('groups', 'aux'), 'atoms'), parts along dimension 0
The draws below stay inside these ranges and needn't reach their ends.
There are 2 independent parts, one for each index of `groups`. The reference program is written for one: setup_inputs(seed, part) draws one part's arguments, and reference() takes and returns one part's arrays. A program takes and returns all parts, laid end to end along the dimension named above; an argument that names none is the same for every part. Nothing has to cross between parts.
Inputs may be any that keep to these rules, and one draw needn't show every extreme that they name: occ_density is symmetric. `partner_list`: each row lists 3 different blocks, the first being the row's own block.
All inputs are finite; a program needn't handle non-finite values.
Results may differ from the reference program's by a relative error of at most 0.005.
Values may be sent and summed in bfloat16 or wider, within the bound.
No kernel may reach another device: no remote copies, remote signals or barrier semaphores. Data moves between devices by JAX's collectives and lax.ppermute only.
A program may use at most 64 MiB of HBM per device.

```python
import math
import jax
import jax.numpy as jnp
import numpy as np
from jax import lax

BS = 128
KN = 3
NBLK = 16
NB = 2048
NAUX = 4


def draw_occ_density(key, part):
    key = jax.random.fold_in(key, 11)
    first_key = jax.random.fold_in(key, 0)
    entries = jax.random.normal(first_key, (NB, NB), jnp.float32)
    paired = (entries + entries.T) * 0.5 ** 0.5 / NB ** 0.5
    return paired.astype(jnp.bfloat16)


def draw_partner_list(key, part):
    key = jax.random.fold_in(key, 7)
    scores = jax.random.randint(key, (NBLK, NBLK), 0, 1 << 20)
    column = jnp.arange(NBLK)[None, :]
    scores = scores * NBLK + column
    scores = jnp.where(column == jnp.arange(NBLK)[:, None], -1, scores)
    ranked = jnp.argsort(scores, axis=1, stable=True)
    return ranked[:, :KN].astype(jnp.int32)


def block_levels(rng, dims, cuts, smallest, largest):
    factor_of, own = 1.0, jax.random.fold_in(rng, 6)
    for axis_at, shards_of in cuts:
        draws = jnp.exp(jax.random.uniform(jax.random.fold_in(own, axis_at), (shards_of,), jnp.float32, smallest / len(cuts), largest / len(cuts)))
        factor_of = factor_of * jnp.repeat(draws, dims[axis_at] // shards_of).reshape([-1 if axis == axis_at else 1 for axis in range(len(dims))])
    return factor_of


def length_profile(number_of, total, most, slope):
    loads = [(1 << 20) // math.isqrt(standing ** slope) + 1 for standing in range(2, number_of + 1)]
    spare, holding = total - most - (number_of - 1), [1] * (number_of - 1)
    while spare > 0:
        free = [i for i in range(number_of - 1) if holding[i] < most]
        pool, remaining = sum([loads[i] for i in free]), spare
        for i in free:
            more = min(most - holding[i], max(1, remaining * loads[i] // pool), spare)
            holding[i] = holding[i] + more
            spare = spare - more
    return np.array([most] + holding)


def uneven(stream_key, count, total, bound, slope):
    if count == 2:
        one = jax.random.randint(stream_key, (), max(1, total - bound), min(bound, total - 1) + 1)
        return jnp.stack([one, total - one])
    sizes = jnp.asarray(length_profile(count, total, bound, slope), jnp.int32)
    twos = (count - 1) // 2
    giver, sink = sizes[1:1 + 2 * twos:2], sizes[2:2 + 2 * twos:2]
    slack = jnp.minimum(giver - 1, bound - sink)
    passed = jax.random.randint(jax.random.fold_in(stream_key, 1), (twos,), 0, 1 << 20) % (slack + 1)
    sizes = sizes.at[1:1 + 2 * twos:2].set(giver - passed).at[2:2 + 2 * twos:2].set(sink + passed)
    return sizes[jax.random.permutation(jax.random.fold_in(stream_key, 2), count)]


def scatter_about(key, shape, width, limit, cuts=(), dtype=jnp.bfloat16):
    factor_of = block_levels(key, shape, cuts, -0.22, 0.18) if cuts else 1.0
    values = jax.random.normal(key, shape, jnp.float32) * width * factor_of
    return jnp.minimum(jnp.maximum(values, -limit), limit).astype(dtype)


def setup_inputs(seed: int = 0, part: int = 0) -> dict:
    streams_of = jax.random.split(jax.random.key(seed), 6)
    part_keys = jax.random.split(jax.random.fold_in(streams_of[5], part), 6)
    return {
        "three_center": scatter_about(streams_of[0], (NB, NAUX, KN, BS), (KN * BS) ** -0.5, 0.3125, ((0, 4), (1, 4))),
        "virt_density": scatter_about(part_keys[1], (NB, NB), 1.0, 6.0, ((0, 4),)),
        "occ_density": draw_occ_density(jax.random.fold_in(jax.random.fold_in(streams_of[5], part), 71), part),
        "partner_list": draw_partner_list(jax.random.fold_in(streams_of[5], 71), part),
        "partner_count": uneven(streams_of[4], NBLK, NBLK * KN * 5 // 8, KN, 1).astype(jnp.int32),
    }


def reference(three_center, virt_density, occ_density, partner_list, partner_count):
    usable = (jnp.arange(KN)[None, :] < partner_count[:, None]).astype(jnp.bfloat16)
    usable_rows = jnp.repeat(usable, BS, axis=0)
    masked = three_center * usable_rows[:, None, :, None]
    masked_flat = masked.reshape(NB, NAUX, KN * BS).astype(jnp.float32)
    picked = virt_density.reshape(NBLK, BS, NB)[partner_list].astype(jnp.float32)
    occ_blocks = occ_density.reshape(NB, NBLK, BS).astype(jnp.float32)

    def one_row(aux_index):
        aux_slab = lax.dynamic_index_in_dim(masked, aux_index, 1, keepdims=False)
        aux_slab = aux_slab.reshape(NBLK, BS, KN, BS).astype(jnp.float32)
        product = jnp.einsum("brkn,bknc->brc", aux_slab, picked).astype(jnp.bfloat16)
        product = product.reshape(NB, NBLK, BS)
        selected = product[:, partner_list].astype(jnp.float32)
        left_side = jnp.einsum("mbr,mbks->brks", occ_blocks, selected).astype(jnp.bfloat16)
        left_flat = left_side.reshape(NB, KN * BS).astype(jnp.float32)
        return jnp.einsum("le,lqe->q", left_flat, masked_flat)

    summed = lax.map(one_row, jnp.arange(NAUX).astype(jnp.int32))
    return summed * jnp.float32(-(NB ** -0.5))
```

```python
import functools

import jax
import jax.numpy as jnp
from jax import lax
from jax.experimental import pallas as pl
from jax.experimental.pallas import tpu as pltpu
from jax.sharding import PartitionSpec as P

BS = 128
KN = 3
MIB = 1 << 20


def swap(x, axes, sizes, move):
    perm = []
    total = 1
    for size in sizes:
        total *= size
    for source in range(total):
        coords, rest = [], source
        for size in reversed(sizes):
            coords.append(rest % size)
            rest //= size
        target = 0
        for size, at in zip(sizes, move(*reversed(coords))):
            target = target * size + at
        perm.append((source, target))
    return lax.ppermute(x, axes, perm)


def contract(n_centers, blocks_here, where, plist, pcount, *refs):
    n_refs = 4 + 8 + 1 + n_centers
    v_refs = refs[0:4]
    m_refs = refs[4:12]
    occ_ref = refs[12]
    c_refs = refs[13:n_refs]
    out_ref = refs[n_refs]
    vbuf, mbuf, obuf, cbuf, prod, acc, vsem, msem, osem, csem = refs[n_refs + 1 :]
    rows = v_refs[0].shape[0]
    pairs = vbuf.shape[0]
    n_blocks = plist.shape[0]
    own = where[0]
    parity = where[1]
    plane = where[2]
    aux_at = where[3]

    def shard_of(i):
        return own ^ i

    def needed(pair):
        hit = jnp.int32(0)
        for b in range(blocks_here):
            block = own * blocks_here + b
            for k in range(KN):
                p = plist[block, k]
                use = (k < pcount[block]) & ((p & 1) == parity) & ((p >> 2) == pair)
                hit = hit | use.astype(jnp.int32)
        return hit > 0

    def v_copy(i, pair):
        return pltpu.make_async_copy(
            v_refs[i].at[:, pl.ds(pl.multiple_of(pair * 2 * BS, 2 * BS), 2 * BS)],
            vbuf.at[pair, pl.ds(pl.multiple_of(shard_of(i) * rows, rows), rows)],
            vsem.at[pair, i],
        )

    def m_copies():
        out = []
        for i in range(8):
            if i in (0, 1, 4, 5):
                slot, shard = i // 4, shard_of(i % 2)
            else:
                slot, shard = (plane if i < 4 else 1 - plane), shard_of(2 + i % 2)
            out.append(
                pltpu.make_async_copy(
                    m_refs[i],
                    mbuf.at[slot, pl.ds(pl.multiple_of(shard * rows, rows), rows)],
                    msem.at[i],
                )
            )
        return out

    def c_copies():
        if n_centers == 1:
            return [pltpu.make_async_copy(c_refs[0], cbuf, csem.at[0])]
        slots = [aux_at, aux_at ^ 1, aux_at ^ (2 | plane), aux_at ^ (3 ^ plane)]
        return [pltpu.make_async_copy(c_refs[i], cbuf.at[slots[i]], csem.at[i]) for i in range(4)]

    for copy in m_copies():
        copy.start()
    for pair in range(pairs):

        @pl.when(needed(pair))
        def _():
            for i in range(4):
                v_copy(i, pair).start()

    o_copy = pltpu.make_async_copy(occ_ref, obuf, osem)
    o_copy.start()
    for copy in c_copies():
        copy.start()
    acc[...] = jnp.zeros_like(acc)
    for copy in m_copies():
        copy.wait()

    n_q = cbuf.shape[0]
    o_copy.wait()
    for copy in c_copies():
        copy.wait()

    def one_pair(pair, carry):
        @pl.when(needed(pair))
        def _():
            for i in range(4):
                v_copy(i, pair).wait()

            def one_block(block, carry):
                row = pl.multiple_of(block * BS, BS)

                def emit(depth):
                    left = jnp.concatenate(
                        [mbuf[s, pl.ds(row, BS), : depth * BS] for s in range(2)], axis=0
                    )
                    right = jnp.concatenate(
                        [
                            vbuf[pair, pl.ds(pl.multiple_of(plist[block, k] * BS, BS), BS), :]
                            for k in range(depth)
                        ],
                        axis=0,
                    )
                    res = jnp.dot(left, right, preferred_element_type=jnp.float32).astype(
                        jnp.bfloat16
                    )
                    for s in range(2):
                        for c in range(2):
                            prod[c, pl.ds(row, BS), s * BS : (s + 1) * BS] = res[
                                s * BS : (s + 1) * BS, c * BS : (c + 1) * BS
                            ]

                for depth in range(1, KN + 1):
                    pl.when(pcount[block] == depth)(functools.partial(emit, depth))
                return carry

            lax.fori_loop(0, n_blocks, one_block, 0)

            for b in range(blocks_here):
                block = own * blocks_here + b
                for k in range(KN):
                    p = plist[block, k]

                    @pl.when((k < pcount[block]) & ((p & 1) == parity) & ((p >> 2) == pair))
                    def _(b=b, k=k, p=p):
                        half = (p >> 1) & 1
                        tile = jnp.dot(
                            obuf[b * BS : (b + 1) * BS, :],
                            prod[half],
                            preferred_element_type=jnp.float32,
                        )
                        tile = tile.astype(jnp.bfloat16).astype(jnp.float32)

                        def add(q):
                            center = cbuf[q, b * BS : (b + 1) * BS, k * BS : (k + 1) * BS]
                            center = center.astype(jnp.float32)
                            for s in range(2):
                                term = tile[:, s * BS : (s + 1) * BS] * center
                                acc[s, q] += term.reshape(BS // 8, 8, BS).sum(axis=0)

                        if n_q <= 8:
                            for q in range(n_q):
                                add(q)
                        else:
                            lax.fori_loop(0, n_q, lambda q, c: (add(q), c)[1], 0)

        return carry

    lax.fori_loop(0, pairs, one_pair, 0)
    for s in range(2):
        out_ref[s] = acc[s].sum(axis=1)


def on_device(sizes, three_center, virt_density, occ_density, partner_list, partner_count):
    groups, aux, atoms = sizes
    rows = three_center.shape[0]
    basis_total = virt_density.shape[1]
    blocks_here = rows // BS
    group_at = lax.axis_index("groups")
    aux_at = lax.axis_index("aux")
    atom_at = lax.axis_index("atoms")
    parity = aux_at & 1

    centers = three_center.reshape(rows, KN * BS)
    striped = virt_density.reshape(rows, basis_total // (2 * BS), 2, BS)
    mine = lax.dynamic_index_in_dim(striped, parity, 2, keepdims=False)
    mine = mine.reshape(rows, basis_total // 2)

    core = functools.partial(swap, axes=("atoms",), sizes=(atoms,), move=lambda t: (t ^ 1,))
    across = functools.partial(swap, axes=("atoms",), sizes=(atoms,), move=lambda t: (t ^ 2,))
    plane = functools.partial(swap, axes=("groups",), sizes=(groups,), move=lambda g: (g ^ 1,))
    pair = functools.partial(swap, axes=("aux",), sizes=(aux,), move=lambda a: (a ^ 1,))

    other = pair(centers)
    v_across = across(mine)
    far_a = swap(
        centers, ("groups", "aux", "atoms"), sizes, lambda g, a, t: (g, a ^ g, t ^ 2)
    )
    if aux == 4:
        rest_a = swap(centers, ("groups", "aux"), (groups, aux), lambda g, a: (g, a ^ (2 | g)))
        rest_b = plane(rest_a)
        all_centers = [centers, other, rest_a, rest_b]
    else:
        all_centers = [lax.all_gather(centers, "aux", axis=0)]
    far_b = plane(far_a)
    v_core = core(mine)
    v_both = core(v_across)
    occ_rows = occ_density.T

    m_parts = [centers, core(centers), far_a, core(far_a), other, core(other), far_b, core(far_b)]
    v_parts = [mine, v_core, v_across, v_both]
    where = jnp.stack([atom_at, parity, group_at, aux_at]).astype(jnp.int32)
    n_in = 13 + len(all_centers)
    anywhere = pl.BlockSpec(memory_space=pl.ANY)
    scalars = pl.BlockSpec(memory_space=pltpu.SMEM)
    n_pairs = basis_total // (4 * BS)
    sums = pl.pallas_call(
        functools.partial(contract, len(all_centers), blocks_here),
        out_shape=jax.ShapeDtypeStruct((2, aux, BS), jnp.float32),
        in_specs=[scalars] * 3 + [anywhere] * n_in,
        out_specs=pl.BlockSpec(memory_space=pltpu.VMEM),
        scratch_shapes=[
            pltpu.VMEM((n_pairs, basis_total, 2 * BS), jnp.bfloat16),
            pltpu.VMEM((2, basis_total, KN * BS), jnp.bfloat16),
            pltpu.VMEM((rows, basis_total), jnp.bfloat16),
            pltpu.VMEM((aux, rows, KN * BS), jnp.bfloat16),
            pltpu.VMEM((2, basis_total, 2 * BS), jnp.bfloat16),
            pltpu.VMEM((2, aux, 8, BS), jnp.float32),
            pltpu.SemaphoreType.DMA((n_pairs, 4)),
            pltpu.SemaphoreType.DMA((8,)),
            pltpu.SemaphoreType.DMA,
            pltpu.SemaphoreType.DMA((4,)),
        ],
        compiler_params=pltpu.CompilerParams(vmem_limit_bytes=56 * MIB),
    )(where, partner_list, partner_count, *v_parts, *m_parts, occ_rows, *all_centers)

    total = sums[0] + pair(sums[1])
    total = total + core(total)
    total = total + across(total)
    share = aux // atoms
    row = lax.dynamic_slice_in_dim(total, atom_at * share, share, 0)
    return (row.sum(axis=1) * jnp.float32(-(basis_total ** (-0.5))))[None, :]


def solution(mesh):
    sizes = tuple(mesh.shape[name] for name in ("groups", "aux", "atoms"))
    in_specs = (
        P("atoms", "aux", None, None),
        P(("groups", "atoms"), None),
        P("groups", "atoms"),
        P(),
        P(),
    )
    out_specs = P(("groups", "aux"), "atoms")
    return jax.shard_map(
        functools.partial(on_device, sizes),
        mesh=mesh,
        in_specs=in_specs,
        out_specs=out_specs,
        check_vma=False,
    )
```

```python
import functools

import jax
import jax.numpy as jnp
from jax import lax
from jax.experimental import pallas as pl
from jax.experimental.pallas import tpu as pltpu
from jax.sharding import PartitionSpec as P

BS = 128
KN = 3
MIB = 1 << 20


def swap(x, axes, sizes, move):
    perm = []
    total = 1
    for size in sizes:
        total *= size
    for source in range(total):
        coords, rest = [], source
        for size in reversed(sizes):
            coords.append(rest % size)
            rest //= size
        target = 0
        for size, at in zip(sizes, move(*reversed(coords))):
            target = target * size + at
        perm.append((source, target))
    return lax.ppermute(x, axes, perm)


def select(blocks_half, where, virt_ref, near_ref, far_ref, buf, sem):
    parity, half = where[1], where[0] >> 1

    def copy(i):
        at = half if i < blocks_half else 1 - half
        block = 2 * (at * blocks_half + i % blocks_half) + parity
        columns = pl.ds(pl.multiple_of(block * BS, BS), BS)
        return pltpu.make_async_copy(virt_ref.at[:, columns], buf.at[i], sem.at[i])

    order = list(range(blocks_half, 2 * blocks_half)) + list(range(blocks_half))
    for i in order:
        copy(i).start()
    for i in order:
        copy(i).wait()
        out_ref = near_ref if i < blocks_half else far_ref
        row = i % blocks_half * BS
        out_ref[row : row + BS, :] = buf[i].T


def contract(n_centers, far_half, where, plist, pcount, *refs):
    v_refs, m_refs, occ_ref = refs[0:4], refs[4:12], refs[12]
    c_refs = refs[13 : 13 + n_centers]
    out_ref, vbuf, prod, acc, vsem = refs[13 + n_centers :]
    own, parity, plane, aux_at = where[0], where[1], where[2], where[3]
    half = 1 - (own >> 1) if far_half else own >> 1
    columns, rows = v_refs[0].shape
    blocks_here = rows // BS
    n_q = acc.shape[1]

    def used(b, k):
        block = own * blocks_here + b
        p = plist[block, k]
        return (k < pcount[block]) & ((p & 1) == parity) & ((p >> 3) == half)

    any_used = jnp.int32(0)
    for b in range(blocks_here):
        for k in range(KN):
            any_used = any_used | used(b, k).astype(jnp.int32)
    acc[...] = jnp.zeros_like(acc)

    @pl.when(any_used > 0)
    def _():
        copies = [pltpu.make_async_copy(v_refs[i], vbuf.at[own ^ i], vsem.at[i]) for i in range(4)]
        for copy in copies:
            copy.start()
        for copy in copies:
            copy.wait()

        for i in range(4):
            first = (own ^ i) * blocks_here
            mine, others = m_refs[i], m_refs[4 + i]
            slot = 0 if i < 2 else plane

            def one_block(j, carry, first=first, mine=mine, others=others, slot=slot):
                block = first + j
                row = pl.ds(pl.multiple_of(j * BS, BS), BS)
                column = pl.ds(pl.multiple_of(block * BS, BS), BS)

                def emit(depth):
                    weights = jnp.concatenate(
                        [
                            jnp.concatenate([m[k, row, :] for k in range(depth)], axis=1)
                            for m in (mine, others)
                        ],
                        axis=0,
                    )
                    parts = []
                    for k in range(depth):
                        p = plist[block, k]
                        at = pl.ds(pl.multiple_of(lax.rem(p, blocks_here) * BS, BS), BS)
                        parts.append(vbuf[p // blocks_here, :, at])
                    res = lax.dot_general(
                        jnp.concatenate(parts, axis=1),
                        weights,
                        (((1,), (1,)), ((), ())),
                        preferred_element_type=jnp.float32,
                    ).astype(jnp.bfloat16)
                    prod[slot, :, column] = res[:, :BS]
                    prod[1 - slot, :, column] = res[:, BS:]

                for depth in range(1, KN + 1):
                    pl.when(pcount[block] == depth)(functools.partial(emit, depth))
                return carry

            lax.fori_loop(0, blocks_here, one_block, 0)

        for b in range(blocks_here):
            for k in range(KN):
                p = plist[own * blocks_here + b, k]

                @pl.when(used(b, k))
                def _(b=b, k=k, p=p):
                    at = pl.ds(pl.multiple_of(((p >> 1) & 3) * BS, BS), BS)
                    both = jnp.concatenate([prod[0, at, :], prod[1, at, :]], axis=0)
                    left = jnp.dot(
                        both, occ_ref[:, b * BS : (b + 1) * BS], preferred_element_type=jnp.float32
                    )
                    left = left.astype(jnp.bfloat16).astype(jnp.float32)
                    left = [left[s * BS : (s + 1) * BS, :].T for s in range(2)]

                    def add(q, center):
                        center = center.astype(jnp.float32)
                        for s in range(2):
                            acc[s, q] += (left[s] * center).reshape(BS // 8, 8, BS).sum(axis=0)

                    span = slice(b * BS, (b + 1) * BS)
                    if n_centers == 1:
                        lax.fori_loop(
                            0, n_q, lambda q, c: (add(q, c_refs[0][q, k, span, :]), c)[1], 0
                        )
                    else:
                        steps = [0, 1, 2 | plane, 3 ^ plane]
                        for step, c_ref in zip(steps, c_refs):
                            add(aux_at ^ step, c_ref[k, span, :])

    for s in range(2):
        out_ref[s] = acc[s].sum(axis=1)


def on_device(sizes, three_center, virt_density, occ_density, partner_list, partner_count):
    groups, aux, atoms = sizes
    rows = three_center.shape[0]
    basis_total = virt_density.shape[1]
    group_at = lax.axis_index("groups")
    aux_at = lax.axis_index("aux")
    atom_at = lax.axis_index("atoms")
    where = jnp.stack([atom_at, aux_at & 1, group_at, aux_at]).astype(jnp.int32)
    half_columns = basis_total // 4
    n_blocks = half_columns // BS

    core = functools.partial(swap, axes=("atoms",), sizes=(atoms,), move=lambda t: (t ^ 1,))
    across = functools.partial(swap, axes=("atoms",), sizes=(atoms,), move=lambda t: (t ^ 2,))
    plane = functools.partial(swap, axes=("groups",), sizes=(groups,), move=lambda g: (g ^ 1,))
    pair = functools.partial(swap, axes=("aux",), sizes=(aux,), move=lambda a: (a ^ 1,))

    anywhere = pl.BlockSpec(memory_space=pl.ANY)
    scalars = pl.BlockSpec(memory_space=pltpu.SMEM)
    vmem = pl.BlockSpec(memory_space=pltpu.VMEM)

    centers = three_center[:, 0].transpose(1, 0, 2)
    far_a = swap(
        centers, ("groups", "aux", "atoms"), sizes, lambda g, a, t: (g, a ^ g, t ^ 2)
    )
    near, far = pl.pallas_call(
        functools.partial(select, n_blocks),
        out_shape=[jax.ShapeDtypeStruct((half_columns, rows), jnp.bfloat16)] * 2,
        in_specs=[scalars, anywhere],
        out_specs=[vmem, vmem],
        scratch_shapes=[
            pltpu.VMEM((2 * n_blocks, rows, BS), jnp.bfloat16),
            pltpu.SemaphoreType.DMA((2 * n_blocks,)),
        ],
        compiler_params=pltpu.CompilerParams(vmem_limit_bytes=8 * MIB),
    )(where, virt_density)

    v_a = across(far)
    other = pair(centers)
    if aux == 4:
        rest_a = swap(centers, ("groups", "aux"), (groups, aux), lambda g, a: (g, a ^ (2 | g)))
    v_b = across(near)
    far_b = plane(far_a)
    if aux == 4:
        rest_b = plane(rest_a)
        all_centers = [centers, other, rest_a, rest_b]
    else:
        all_centers = [lax.all_gather(centers, "aux", axis=0)]

    m_parts = [centers, core(centers), far_a, core(far_a), other, core(other), far_b, core(far_b)]

    def run(far_half, v_parts):
        return pl.pallas_call(
            functools.partial(contract, len(all_centers), far_half),
            out_shape=jax.ShapeDtypeStruct((2, aux, BS), jnp.float32),
            in_specs=[scalars] * 3 + [anywhere] * 4 + [vmem] * (9 + len(all_centers)),
            out_specs=vmem,
            scratch_shapes=[
                pltpu.VMEM((4, half_columns, rows), jnp.bfloat16),
                pltpu.VMEM((2, half_columns, basis_total), jnp.bfloat16),
                pltpu.VMEM((2, aux, 8, BS), jnp.float32),
                pltpu.SemaphoreType.DMA((4,)),
            ],
            compiler_params=pltpu.CompilerParams(
                vmem_limit_bytes=(16 if aux == 4 else 40) * MIB
            ),
        )(where, partner_list, partner_count, *v_parts, *m_parts, occ_density, *all_centers)

    sums = run(False, [near, core(near), v_a, core(v_a)])
    sums = sums + run(True, [far, core(far), v_b, core(v_b)])

    sums = sums + core(sums)
    diagonal = swap(sums[1], ("aux", "atoms"), (aux, atoms), lambda a, t: (a ^ 1, t ^ 2))
    total = sums[0] + across(sums[0]) + pair(sums[1]) + diagonal
    share = aux // atoms
    row = lax.dynamic_slice_in_dim(total, atom_at * share, share, 0)
    return (row.sum(axis=1) * jnp.float32(-(basis_total ** (-0.5))))[None, :]


def solution(mesh):
    sizes = tuple(mesh.shape[name] for name in ("groups", "aux", "atoms"))
    in_specs = (
        P("atoms", "aux", None, None),
        P(("groups", "atoms"), None),
        P("groups", "atoms"),
        P(),
        P(),
    )
    out_specs = P(("groups", "aux"), "atoms")
    return jax.shard_map(
        functools.partial(on_device, sizes),
        mesh=mesh,
        in_specs=in_specs,
        out_specs=out_specs,
        check_vma=False,
    )
```

```python
import functools

import jax
import jax.numpy as jnp
from jax import lax
from jax.experimental import pallas as pl
from jax.experimental.pallas import tpu as pltpu
from jax.sharding import PartitionSpec as P

BS = 128
KN = 3
MIB = 1 << 20


def swap(x, axes, sizes, move):
    perm = []
    total = 1
    for size in sizes:
        total *= size
    for source in range(total):
        coords, rest = [], source
        for size in reversed(sizes):
            coords.append(rest % size)
            rest //= size
        target = 0
        for size, at in zip(sizes, move(*reversed(coords))):
            target = target * size + at
        perm.append((source, target))
    return lax.ppermute(x, axes, perm)


def select(blocks_half, where, virt_ref, near_ref, far_ref, buf, sem):
    parity, half = where[1], where[0] >> 1

    def copy(i):
        at = half if i < blocks_half else 1 - half
        block = 2 * (at * blocks_half + i % blocks_half) + parity
        columns = pl.ds(pl.multiple_of(block * BS, BS), BS)
        return pltpu.make_async_copy(virt_ref.at[:, columns], buf.at[i], sem.at[i])

    order = list(range(blocks_half, 2 * blocks_half)) + list(range(blocks_half))
    for i in order:
        copy(i).start()
    for i in order:
        copy(i).wait()
        out_ref = near_ref if i < blocks_half else far_ref
        row = i % blocks_half * BS
        out_ref[row : row + BS, :] = buf[i].T


def after(x, *others):
    return lax.optimization_barrier((x,) + others)[0]


def left_tiles(far_half, where, plist, pcount, v_refs, m_refs, occ_ref, left_ref, scratch):
    vbuf, mbuf, obuf, prod, listed, place, vsem, msem, osem = scratch
    own, parity = where[0], where[1]
    half = 1 - (own >> 1) if far_half else own >> 1
    basis = mbuf.shape[2]
    rows = basis // 4
    blocks_here = rows // BS
    n_places = vbuf.shape[0]

    def used(b, k):
        block = own * blocks_here + b
        p = plist[block, k]
        return (k < pcount[block]) & ((p & 1) == parity) & ((p >> 3) == half)

    def column(b, k):
        return (plist[own * blocks_here + b, k] >> 1) & 3

    count = jnp.int32(0)
    for c in range(n_places):
        need = jnp.int32(0)
        for b in range(blocks_here):
            for k in range(KN):
                need = need | (used(b, k) & (column(b, k) == c)).astype(jnp.int32)
        place[c] = count

        @pl.when(need > 0)
        def _(c=c, count=count):
            listed[count] = c

        count = count + need

    @pl.when((count & 1) == 1)
    def _():
        listed[count] = listed[count - 1]

    groups = (count + 1) >> 1

    def v_copies(at):
        row = pl.ds(pl.multiple_of(listed[at] * BS, BS), BS)
        return [
            pltpu.make_async_copy(v_refs[i].at[row], vbuf.at[at, own ^ i], vsem.at[at, i])
            for i in range(4)
        ]

    def m_copies():
        out = []
        for i in range(8):
            span = pl.ds(pl.multiple_of((own ^ (i % 4)) * rows, rows), rows)
            out.append(
                pltpu.make_async_copy(m_refs[i], mbuf.at[i // 4, :, span], msem.at[i])
            )
        return out

    o_copy = pltpu.make_async_copy(occ_ref, obuf, osem)

    @pl.when(count > 0)
    def _():
        for copy in v_copies(0) + v_copies(1) + m_copies():
            copy.start()

        @pl.when(groups > 1)
        def _():
            for copy in v_copies(2) + v_copies(3):
                copy.start()

        o_copy.start()
        for copy in m_copies():
            copy.wait()

        def one_group(g, carry):
            for copy in v_copies(2 * g) + v_copies(2 * g + 1):
                copy.wait()

            def four_blocks(i, carry):
                for j in range(4):
                    block = 4 * i + j
                    span = pl.ds(pl.multiple_of(block * BS, BS), BS)
                    weights, parts = [], []
                    for k in range(KN):
                        p = plist[block, k]
                        at = pl.ds(pl.multiple_of((p & 3) * BS, BS), BS)
                        parts.append(
                            jnp.concatenate(
                                [vbuf[2 * g + h, p >> 2, :, at] for h in range(2)], axis=0
                            )
                        )
                        weight = jnp.concatenate([mbuf[s, k, span, :] for s in range(2)], axis=0)
                        if k > 0:
                            weight = jnp.where(k < pcount[block], weight, jnp.zeros_like(weight))
                        weights.append(weight)
                    res = lax.dot_general(
                        jnp.concatenate(parts, axis=1),
                        jnp.concatenate(weights, axis=1),
                        (((1,), (1,)), ((), ())),
                        preferred_element_type=jnp.float32,
                    ).astype(jnp.bfloat16)
                    for s in range(2):
                        for h in range(2):
                            prod[2 * g + h, s * BS : (s + 1) * BS, span] = res[
                                h * BS : (h + 1) * BS, s * BS : (s + 1) * BS
                            ]
                return carry

            lax.fori_loop(0, basis // (4 * BS), four_blocks, 0)
            return carry

        lax.fori_loop(0, groups, one_group, 0)
        o_copy.wait()
        for b in range(blocks_here):
            for k in range(KN):

                @pl.when(used(b, k))
                def _(b=b, k=k):
                    left = jnp.dot(
                        prod[place[column(b, k)]],
                        obuf[:, b * BS : (b + 1) * BS],
                        preferred_element_type=jnp.float32,
                    )
                    left_ref[b * KN + k] = left.astype(jnp.bfloat16)


def first(where, plist, pcount, *refs):
    left_tiles(False, where, plist, pcount, refs[0:4], refs[4:12], refs[12], refs[13], refs[14:])


def second(n_centers, where, plist, pcount, *refs):
    before_ref = refs[13]
    c_refs = refs[14 : 14 + n_centers]
    out_ref, left, cbuf, acc, csem, bsem = refs[14 + n_centers : 20 + n_centers]
    own, parity, plane, aux_at = where[0], where[1], where[2], where[3]
    half = 1 - (own >> 1)
    n_q, _, rows, _ = cbuf.shape
    blocks_here = rows // BS

    if n_centers == 1:
        copies = [pltpu.make_async_copy(c_refs[0], cbuf, csem.at[0])]
    else:
        steps = [0, 1, 2 | plane, 3 ^ plane]
        copies = [
            pltpu.make_async_copy(c_refs[i], cbuf.at[aux_at ^ steps[i]], csem.at[i])
            for i in range(n_centers)
        ]
    slots = [(b, k) for b in range(blocks_here) for k in range(KN)]

    def kept(b, k):
        block = own * blocks_here + b
        p = plist[block, k]
        return (k < pcount[block]) & ((p & 1) == parity) & ((p >> 3) != half)

    def before(b, k):
        i = b * KN + k
        return pltpu.make_async_copy(before_ref.at[i], left.at[i], bsem.at[i])

    for b, k in slots:
        pl.when(kept(b, k))(lambda b=b, k=k: before(b, k).start())
    for copy in copies:
        copy.start()
    acc[...] = jnp.zeros_like(acc)
    left_tiles(
        True, where, plist, pcount, refs[0:4], refs[4:12], refs[12], left, refs[20 + n_centers :]
    )
    for b, k in slots:
        pl.when(kept(b, k))(lambda b=b, k=k: before(b, k).wait())
    for copy in copies:
        copy.wait()

    for b, k in slots:
        block = own * blocks_here + b

        @pl.when((k < pcount[block]) & ((plist[block, k] & 1) == parity))
        def _(b=b, k=k):
            tile = left[b * KN + k].astype(jnp.float32)
            tile = [tile[s * BS : (s + 1) * BS, :].T for s in range(2)]

            def add(q, carry):
                center = cbuf[q, k, b * BS : (b + 1) * BS, :].astype(jnp.float32)
                for s in range(2):
                    acc[s, q] += (tile[s] * center).reshape(BS // 8, 8, BS).sum(axis=0)
                return carry

            lax.fori_loop(0, n_q, add, 0, unroll=n_q <= 8)

    for s in range(2):
        out_ref[s] = acc[s].sum(axis=1)


def on_device(sizes, three_center, virt_density, occ_density, partner_list, partner_count):
    groups, aux, atoms = sizes
    rows = three_center.shape[0]
    basis_total = virt_density.shape[1]
    group_at = lax.axis_index("groups")
    aux_at = lax.axis_index("aux")
    atom_at = lax.axis_index("atoms")
    where = jnp.stack([atom_at, aux_at & 1, group_at, aux_at]).astype(jnp.int32)
    half_columns = basis_total // 4
    n_blocks = half_columns // BS
    n_slots = rows // BS * KN

    core = functools.partial(swap, axes=("atoms",), sizes=(atoms,), move=lambda t: (t ^ 1,))
    across = functools.partial(swap, axes=("atoms",), sizes=(atoms,), move=lambda t: (t ^ 2,))
    plane = functools.partial(swap, axes=("groups",), sizes=(groups,), move=lambda g: (g ^ 1,))
    pair = functools.partial(swap, axes=("aux",), sizes=(aux,), move=lambda a: (a ^ 1,))

    anywhere = pl.BlockSpec(memory_space=pltpu.HBM)
    scalars = pl.BlockSpec(memory_space=pltpu.SMEM)
    vmem = pl.BlockSpec(memory_space=pltpu.VMEM)

    centers = three_center[:, 0].transpose(1, 0, 2)
    far_a = across(centers)
    other = pair(centers)
    near, far = pl.pallas_call(
        functools.partial(select, n_blocks),
        out_shape=[jax.ShapeDtypeStruct((half_columns, rows), jnp.bfloat16)] * 2,
        in_specs=[scalars, anywhere],
        out_specs=[vmem, vmem],
        scratch_shapes=[
            pltpu.VMEM((2 * n_blocks, rows, BS), jnp.bfloat16),
            pltpu.SemaphoreType.DMA((2 * n_blocks,)),
        ],
        compiler_params=pltpu.CompilerParams(vmem_limit_bytes=8 * MIB),
    )(where, virt_density)
    v_a = across(far)
    if aux == 4:
        rest_a = swap(centers, ("groups", "aux"), (groups, aux), lambda g, a: (g, a ^ (2 | g)))
        rest_b = plane(rest_a)
        all_centers = [centers, other, rest_a, rest_b]
        early, late = rest_a, rest_b
    else:
        all_centers = [lax.all_gather(centers, "aux", axis=0)]
        early, late = other, all_centers[0]
    far_b = pair(far_a)
    v_b = across(after(near, far_a))

    m_parts = [centers, core(centers), far_a, core(far_a), other, core(other), far_b, core(after(far_b, early))]

    def scratch():
        return [
            pltpu.VMEM((n_blocks, 4, BS, rows), jnp.bfloat16),
            pltpu.VMEM((2, KN, basis_total, BS), jnp.bfloat16),
            pltpu.VMEM((basis_total, rows), jnp.bfloat16),
            pltpu.VMEM((n_blocks, 2 * BS, basis_total), jnp.bfloat16),
            pltpu.SMEM((n_blocks,), jnp.int32),
            pltpu.SMEM((n_blocks,), jnp.int32),
            pltpu.SemaphoreType.DMA((n_blocks, 4)),
            pltpu.SemaphoreType.DMA((8,)),
            pltpu.SemaphoreType.DMA,
        ]

    tiles = jax.ShapeDtypeStruct((n_slots, 2 * BS, BS), jnp.bfloat16)
    before = pl.pallas_call(
        first,
        out_shape=tiles,
        in_specs=[scalars] * 3 + [anywhere] * 13,
        out_specs=vmem,
        scratch_shapes=scratch(),
        compiler_params=pltpu.CompilerParams(vmem_limit_bytes=20 * MIB),
    )(where, partner_list, partner_count, near, core(near), v_a, core(v_a), *m_parts, occ_density)
    v_b_core = core(after(v_b, before, late))
    sums = pl.pallas_call(
        functools.partial(second, len(all_centers)),
        out_shape=jax.ShapeDtypeStruct((2, aux, BS), jnp.float32),
        in_specs=[scalars] * 3 + [anywhere] * (14 + len(all_centers)),
        out_specs=vmem,
        scratch_shapes=[
            pltpu.VMEM(tiles.shape, tiles.dtype),
            pltpu.VMEM((aux, KN, rows, BS), jnp.bfloat16),
            pltpu.VMEM((2, aux, 8, BS), jnp.float32),
            pltpu.SemaphoreType.DMA((4,)),
            pltpu.SemaphoreType.DMA((n_slots,)),
        ]
        + scratch(),
        compiler_params=pltpu.CompilerParams(vmem_limit_bytes=(20 if aux == 4 else 48) * MIB),
    )(
        where,
        partner_list,
        partner_count,
        far,
        core(far),
        v_b,
        v_b_core,
        *m_parts,
        occ_density,
        before,
        *all_centers,
    )

    sums = sums + core(sums)
    diagonal = swap(sums[1], ("aux", "atoms"), (aux, atoms), lambda a, t: (a ^ 1, t ^ 2))
    total = sums[0] + across(sums[0]) + pair(sums[1]) + diagonal
    share = aux // atoms
    row = lax.dynamic_slice_in_dim(total, atom_at * share, share, 0)
    return (row.sum(axis=1) * jnp.float32(-(basis_total ** (-0.5))))[None, :]


def solution(mesh):
    sizes = tuple(mesh.shape[name] for name in ("groups", "aux", "atoms"))
    in_specs = (
        P("atoms", "aux", None, None),
        P(("groups", "atoms"), None),
        P("groups", "atoms"),
        P(),
        P(),
    )
    out_specs = P(("groups", "aux"), "atoms")
    return jax.shard_map(
        functools.partial(on_device, sizes),
        mesh=mesh,
        in_specs=in_specs,
        out_specs=out_specs,
        check_vma=False,
    )
```

```python
import functools

import jax
import jax.numpy as jnp
from jax import lax
from jax.experimental import pallas as pl
from jax.experimental.pallas import tpu as pltpu
from jax.sharding import PartitionSpec as P

BS = 128
KN = 3
MIB = 1 << 20


def swap(x, axes, sizes, move):
    perm = []
    total = 1
    for size in sizes:
        total *= size
    for source in range(total):
        coords, rest = [], source
        for size in reversed(sizes):
            coords.append(rest % size)
            rest //= size
        target = 0
        for size, at in zip(sizes, move(*reversed(coords))):
            target = target * size + at
        perm.append((source, target))
    return lax.ppermute(x, axes, perm)


def select(n_blocks, where, virt_ref, out_ref, buf, sem):
    def copy(i):
        columns = pl.ds(pl.multiple_of((2 * i + where[1]) * BS, BS), BS)
        return pltpu.make_async_copy(virt_ref.at[:, columns], buf.at[i], sem.at[i])

    for i in range(n_blocks):
        copy(i).start()
    for i in range(n_blocks):
        copy(i).wait()
        out_ref[i * BS : (i + 1) * BS, :] = buf[i].T


def after(x, *others):
    return lax.optimization_barrier((x,) + others)[0]


def contract(n_centers, where, plist, pcount, *refs):
    v_refs, m_refs, occ_ref, c_refs = refs[0:4], refs[4:12], refs[12], refs[13 : 13 + n_centers]
    out_ref = refs[13 + n_centers]
    vbuf, mbuf, obuf, cbuf, prod, acc, listed, place, vsem, msem, osem, csem = refs[
        14 + n_centers :
    ]
    own, parity, plane, aux_at = where[0], where[1], where[2], where[3]
    basis = mbuf.shape[2]
    n_q, _, rows, _ = cbuf.shape
    blocks_here = rows // BS
    n_places = vbuf.shape[0]
    slots = [(b, k) for b in range(blocks_here) for k in range(KN)]

    def used(b, k):
        block = own * blocks_here + b
        return (k < pcount[block]) & ((plist[block, k] & 1) == parity)

    def column(b, k):
        return plist[own * blocks_here + b, k] >> 1

    for c in range(n_places):
        place[c] = -1
    count = jnp.int32(0)
    for k in range(KN):
        for b in range(blocks_here):
            c = column(b, k)
            new = used(b, k) & (place[c] < 0)

            @pl.when(new)
            def _(c=c, count=count):
                place[c] = count
                listed[count] = c

            count = count + new.astype(jnp.int32)

    @pl.when((count & 1) == 1)
    def _():
        listed[count] = listed[count - 1]

    groups = (count + 1) >> 1

    def v_copies(at):
        row = pl.ds(pl.multiple_of(listed[at] * BS, BS), BS)
        return [
            pltpu.make_async_copy(v_refs[i].at[row], vbuf.at[at, own ^ i], vsem.at[at, i])
            for i in range(4)
        ]

    def m_copies():
        out = []
        for i in range(8):
            span = pl.ds(pl.multiple_of((own ^ (i % 4)) * rows, rows), rows)
            out.append(pltpu.make_async_copy(m_refs[i], mbuf.at[i // 4, :, span], msem.at[i]))
        return out

    o_copy = pltpu.make_async_copy(occ_ref, obuf, osem)
    if n_centers == 1:
        c_copies = [pltpu.make_async_copy(c_refs[0], cbuf, csem.at[0])]
    else:
        steps = [0, 1, 2 | plane, 3 ^ plane]
        c_copies = [
            pltpu.make_async_copy(c_refs[i], cbuf.at[aux_at ^ steps[i]], csem.at[i])
            for i in range(n_centers)
        ]

    for copy in v_copies(0) + v_copies(1) + m_copies():
        copy.start()
    for g in range(1, n_places // 2):

        @pl.when(g < groups)
        def _(g=g):
            for copy in v_copies(2 * g) + v_copies(2 * g + 1):
                copy.start()

    o_copy.start()
    for copy in c_copies:
        copy.start()
    acc[...] = jnp.zeros_like(acc)
    for copy in m_copies():
        copy.wait()

    def one_group(g, carry):
        for copy in v_copies(2 * g) + v_copies(2 * g + 1):
            copy.wait()

        def four_blocks(i, carry):
            for j in range(4):
                block = 4 * i + j
                span = pl.ds(pl.multiple_of(block * BS, BS), BS)
                weights, parts = [], []
                for k in range(KN):
                    p = plist[block, k]
                    at = pl.ds(pl.multiple_of((p & 3) * BS, BS), BS)
                    parts.append(
                        jnp.concatenate([vbuf[2 * g + h, p >> 2, :, at] for h in range(2)], axis=0)
                    )
                    weight = jnp.concatenate([mbuf[s, k, span, :] for s in range(2)], axis=0)
                    if k > 0:
                        weight = jnp.where(k < pcount[block], weight, jnp.zeros_like(weight))
                    weights.append(weight)
                res = lax.dot_general(
                    jnp.concatenate(parts, axis=1),
                    jnp.concatenate(weights, axis=1),
                    (((1,), (1,)), ((), ())),
                    preferred_element_type=jnp.float32,
                ).astype(jnp.bfloat16)
                for s in range(2):
                    for h in range(2):
                        prod[2 * g + h, s * BS : (s + 1) * BS, span] = res[
                            h * BS : (h + 1) * BS, s * BS : (s + 1) * BS
                        ]
            return carry

        lax.fori_loop(0, basis // (4 * BS), four_blocks, 0)
        return carry

    lax.fori_loop(0, groups, one_group, 0)
    o_copy.wait()
    for copy in c_copies:
        copy.wait()

    for b, k in slots:

        @pl.when(used(b, k))
        def _(b=b, k=k):
            left = jnp.dot(
                prod[place[column(b, k)]],
                obuf[:, b * BS : (b + 1) * BS],
                preferred_element_type=jnp.float32,
            )
            left = left.astype(jnp.bfloat16).astype(jnp.float32)
            left = [left[s * BS : (s + 1) * BS, :].T for s in range(2)]

            def add(q, carry):
                center = cbuf[q, k, b * BS : (b + 1) * BS, :].astype(jnp.float32)
                for s in range(2):
                    acc[s, q] += (left[s] * center).reshape(BS // 8, 8, BS).sum(axis=0)
                return carry

            lax.fori_loop(0, n_q, add, 0, unroll=n_q <= 8)

    for s in range(2):
        out_ref[s] = acc[s].sum(axis=1)


def on_device(sizes, three_center, virt_density, occ_density, partner_list, partner_count):
    groups, aux, atoms = sizes
    rows = three_center.shape[0]
    basis_total = virt_density.shape[1]
    group_at = lax.axis_index("groups")
    aux_at = lax.axis_index("aux")
    atom_at = lax.axis_index("atoms")
    where = jnp.stack([atom_at, aux_at & 1, group_at, aux_at]).astype(jnp.int32)
    columns = basis_total // 2
    n_blocks = columns // BS

    core = functools.partial(swap, axes=("atoms",), sizes=(atoms,), move=lambda t: (t ^ 1,))
    across = functools.partial(swap, axes=("atoms",), sizes=(atoms,), move=lambda t: (t ^ 2,))
    plane = functools.partial(swap, axes=("groups",), sizes=(groups,), move=lambda g: (g ^ 1,))
    pair = functools.partial(swap, axes=("aux",), sizes=(aux,), move=lambda a: (a ^ 1,))

    anywhere = pl.BlockSpec(memory_space=pltpu.HBM)
    scalars = pl.BlockSpec(memory_space=pltpu.SMEM)
    vmem = pl.BlockSpec(memory_space=pltpu.VMEM)

    centers = three_center[:, 0].transpose(1, 0, 2)
    far_a = across(centers)
    other = pair(centers)
    mine = pl.pallas_call(
        functools.partial(select, n_blocks),
        out_shape=jax.ShapeDtypeStruct((columns, rows), jnp.bfloat16),
        in_specs=[scalars, anywhere],
        out_specs=vmem,
        scratch_shapes=[
            pltpu.VMEM((n_blocks, rows, BS), jnp.bfloat16),
            pltpu.SemaphoreType.DMA((n_blocks,)),
        ],
        compiler_params=pltpu.CompilerParams(vmem_limit_bytes=8 * MIB),
    )(where, virt_density)
    v_across = across(mine)
    far_b = pair(after(far_a, other))
    if aux == 4:
        rest_a = swap(centers, ("groups", "aux"), (groups, aux), lambda g, a: (g, a ^ (2 | g)))
        rest_b = plane(rest_a)
        all_centers = [centers, other, rest_a, rest_b]
    else:
        all_centers = [lax.all_gather(centers, "aux", axis=0)]

    m_parts = [centers, core(centers), far_a, core(far_a), other, core(other), far_b]
    m_parts.append(core(far_b))
    v_parts = [mine, core(mine), v_across, core(after(v_across, *m_parts[1:], all_centers[-1]))]

    sums = pl.pallas_call(
        functools.partial(contract, len(all_centers)),
        out_shape=jax.ShapeDtypeStruct((2, aux, BS), jnp.float32),
        in_specs=[scalars] * 3 + [anywhere] * (13 + len(all_centers)),
        out_specs=vmem,
        scratch_shapes=[
            pltpu.VMEM((n_blocks, 4, BS, rows), jnp.bfloat16),
            pltpu.VMEM((2, KN, basis_total, BS), jnp.bfloat16),
            pltpu.VMEM((basis_total, rows), jnp.bfloat16),
            pltpu.VMEM((aux, KN, rows, BS), jnp.bfloat16),
            pltpu.VMEM((n_blocks, 2 * BS, basis_total), jnp.bfloat16),
            pltpu.VMEM((2, aux, 8, BS), jnp.float32),
            pltpu.SMEM((n_blocks,), jnp.int32),
            pltpu.SMEM((n_blocks,), jnp.int32),
            pltpu.SemaphoreType.DMA((n_blocks, 4)),
            pltpu.SemaphoreType.DMA((8,)),
            pltpu.SemaphoreType.DMA,
            pltpu.SemaphoreType.DMA((4,)),
        ],
        compiler_params=pltpu.CompilerParams(vmem_limit_bytes=58 * MIB),
    )(where, partner_list, partner_count, *v_parts, *m_parts, occ_density, *all_centers)

    sums = sums + core(sums)
    diagonal = swap(sums[1], ("aux", "atoms"), (aux, atoms), lambda a, t: (a ^ 1, t ^ 2))
    total = sums[0] + across(sums[0]) + pair(sums[1]) + diagonal
    share = aux // atoms
    row = lax.dynamic_slice_in_dim(total, atom_at * share, share, 0)
    return (row.sum(axis=1) * jnp.float32(-(basis_total ** (-0.5))))[None, :]


def solution(mesh):
    sizes = tuple(mesh.shape[name] for name in ("groups", "aux", "atoms"))
    in_specs = (
        P("atoms", "aux", None, None),
        P(("groups", "atoms"), None),
        P("groups", "atoms"),
        P(),
        P(),
    )
    out_specs = P(("groups", "aux"), "atoms")
    return jax.shard_map(
        functools.partial(on_device, sizes),
        mesh=mesh,
        in_specs=in_specs,
        out_specs=out_specs,
        check_vma=False,
    )
```

```python
import functools

import jax
import jax.numpy as jnp
from jax import lax
from jax.experimental import pallas as pl
from jax.experimental.pallas import tpu as pltpu
from jax.sharding import PartitionSpec as P

BS = 128
KN = 3
MIB = 1 << 20


def swap(x, axes, sizes, move):
    perm = []
    total = 1
    for size in sizes:
        total *= size
    for source in range(total):
        coords, rest = [], source
        for size in reversed(sizes):
            coords.append(rest % size)
            rest //= size
        target = 0
        for size, at in zip(sizes, move(*reversed(coords))):
            target = target * size + at
        perm.append((source, target))
    return lax.ppermute(x, axes, perm)


def select(n_blocks, where, virt_ref, out_ref, buf, sem):
    def copy(i):
        columns = pl.ds(pl.multiple_of((2 * i + where[1]) * BS, BS), BS)
        return pltpu.make_async_copy(virt_ref.at[:, columns], buf.at[i], sem.at[i])

    for i in range(n_blocks):
        copy(i).start()
    for i in range(n_blocks):
        copy(i).wait()
        out_ref[i * BS : (i + 1) * BS, :] = buf[i].T


def after(x, *others):
    return lax.optimization_barrier((x,) + others)[0]


def stage(n_early, where, pcount, *refs):
    m_refs, occ_ref, c_refs = refs[0:8], refs[8], refs[9 : 9 + n_early]
    packed_ref, occ_rows_ref, centers_ref, flag_ref, mbuf, obuf, msem, osem, csem = refs[9 + n_early :]
    own, plane, aux_at = where[0], where[2], where[3]
    rows = occ_ref.shape[1]
    blocks_here = rows // BS
    m_copies = [pltpu.make_async_copy(m_refs[i], mbuf.at[i], msem.at[i]) for i in range(8)]
    o_copy = pltpu.make_async_copy(occ_ref, obuf, osem)
    steps = [0, 1, 2 | plane][:n_early]
    c_copies = [
        pltpu.make_async_copy(c_refs[i], centers_ref.at[aux_at ^ steps[i]], csem.at[i])
        for i in range(n_early)
    ]
    for copy in m_copies + [o_copy] + c_copies:
        copy.start()
    for i in range(8):
        m_copies[i].wait()
        at = i // 4 * BS
        for j in range(blocks_here):
            block = (own ^ (i % 4)) * blocks_here + j
            for k in range(KN):
                tile = mbuf[i, k, j * BS : (j + 1) * BS, :]
                if k > 0:
                    tile = jnp.where(k < pcount[block], tile, jnp.zeros_like(tile))
                packed_ref[block, at : at + BS, k * BS : (k + 1) * BS] = tile
    o_copy.wait()
    for b in range(blocks_here):
        occ_rows_ref[b * BS : (b + 1) * BS, :] = obuf[:, b * BS : (b + 1) * BS].T
    for copy in c_copies:
        copy.wait()
    flag_ref[...] = jnp.zeros_like(flag_ref)


def contract(n_centers, where, plist, pcount, *refs):
    v_refs, packed_ref, occ_ref, centers_ref = refs[0:4], refs[4], refs[5], refs[6]
    last_ref, out_ref = refs[7], refs[9]
    vbuf, prod, acc, listed, place, vsem = refs[-6:]
    own, parity, plane, aux_at = where[0], where[1], where[2], where[3]
    n_q = acc.shape[1]
    rows = v_refs[0].shape[1]
    blocks_here = rows // BS
    n_places = vbuf.shape[0]
    slots = [(b, k) for b in range(blocks_here) for k in range(KN)]

    def used(b, k):
        block = own * blocks_here + b
        return (k < pcount[block]) & ((plist[k, block] & 1) == parity)

    def column(b, k):
        return plist[k, own * blocks_here + b] >> 1

    for c in range(n_places):
        place[c] = -1
    count = jnp.int32(0)
    for k in range(KN):
        for b in range(blocks_here):
            c = column(b, k)
            new = used(b, k) & (place[c] < 0)

            @pl.when(new)
            def _(c=c, count=count):
                place[c] = count
                listed[count] = c

            count = count + new.astype(jnp.int32)

    @pl.when((count & 1) == 1)
    def _():
        listed[count] = listed[count - 1]

    groups = (count + 1) >> 1

    def v_copies(at):
        row = pl.ds(pl.multiple_of(listed[at] * BS, BS), BS)
        return [
            pltpu.make_async_copy(v_refs[i].at[row], vbuf.at[at, own ^ i], vsem.at[at, i])
            for i in range(4)
        ]

    for copy in v_copies(0) + v_copies(1):
        copy.start()
    for g in range(1, n_places // 2):

        @pl.when(g < groups)
        def _(g=g):
            for copy in v_copies(2 * g) + v_copies(2 * g + 1):
                copy.start()

    acc[...] = jnp.zeros_like(acc)

    def one_group(g, carry):
        for copy in v_copies(2 * g) + v_copies(2 * g + 1):
            copy.wait()

        def four_blocks(i, carry):
            for j in range(4):
                block = 4 * i + j
                parts = []
                for k in range(KN):
                    p = plist[k, block]
                    at = pl.ds(pl.multiple_of((p & 3) * BS, BS), BS)
                    parts.append(
                        jnp.concatenate([vbuf[2 * g + h, p >> 2, :, at] for h in range(2)], axis=0)
                    )
                res = lax.dot_general(
                    jnp.concatenate(parts, axis=1),
                    packed_ref[block],
                    (((1,), (1,)), ((), ())),
                    preferred_element_type=jnp.float32,
                ).astype(jnp.bfloat16)
                span = pl.ds(pl.multiple_of(block * BS, BS), BS)
                for s in range(2):
                    for h in range(2):
                        prod[2 * g + h, s * BS : (s + 1) * BS, span] = res[
                            h * BS : (h + 1) * BS, s * BS : (s + 1) * BS
                        ]
            return carry

        lax.fori_loop(0, packed_ref.shape[0] // 4, four_blocks, 0)
        return carry

    lax.fori_loop(0, groups, one_group, 0)

    for b, k in slots:

        @pl.when(used(b, k))
        def _(b=b, k=k):
            left = lax.dot_general(
                occ_ref[b * BS : (b + 1) * BS, :],
                prod[place[column(b, k)]],
                (((1,), (1,)), ((), ())),
                preferred_element_type=jnp.float32,
            )
            left = left.astype(jnp.bfloat16).astype(jnp.float32)

            def add(q, center):
                center = center.astype(jnp.float32)
                for s in range(2):
                    term = left[:, s * BS : (s + 1) * BS] * center
                    acc[s, q] += term.reshape(BS // 8, 8, BS).sum(axis=0)

            span = slice(b * BS, (b + 1) * BS)
            if n_centers == 1:
                lax.fori_loop(0, n_q, lambda q, x: (add(q, last_ref[q, k, span, :]), x)[1], 0)
            else:
                for step in (0, 1, 2 | plane):
                    add(aux_at ^ step, centers_ref[aux_at ^ step, k, span, :])
                add(aux_at ^ 3 ^ plane, last_ref[k, span, :])

    for s in range(2):
        out_ref[s] = acc[s].sum(axis=1)


def on_device(sizes, three_center, virt_density, occ_density, partner_list, partner_count):
    groups, aux, atoms = sizes
    rows = three_center.shape[0]
    basis_total = virt_density.shape[1]
    group_at = lax.axis_index("groups")
    aux_at = lax.axis_index("aux")
    atom_at = lax.axis_index("atoms")
    where = jnp.stack([atom_at, aux_at & 1, group_at, aux_at]).astype(jnp.int32)
    columns = basis_total // 2
    n_blocks = columns // BS

    core = functools.partial(swap, axes=("atoms",), sizes=(atoms,), move=lambda t: (t ^ 1,))
    across = functools.partial(swap, axes=("atoms",), sizes=(atoms,), move=lambda t: (t ^ 2,))
    plane = functools.partial(swap, axes=("groups",), sizes=(groups,), move=lambda g: (g ^ 1,))
    pair = functools.partial(swap, axes=("aux",), sizes=(aux,), move=lambda a: (a ^ 1,))

    anywhere = pl.BlockSpec(memory_space=pltpu.HBM)
    scalars = pl.BlockSpec(memory_space=pltpu.SMEM)
    vmem = pl.BlockSpec(memory_space=pltpu.VMEM)

    centers = three_center[:, 0].transpose(1, 0, 2)
    far_a = across(centers)
    other = pair(centers)
    mine = pl.pallas_call(
        functools.partial(select, n_blocks),
        out_shape=jax.ShapeDtypeStruct((columns, rows), jnp.bfloat16),
        in_specs=[scalars, anywhere],
        out_specs=vmem,
        scratch_shapes=[
            pltpu.VMEM((n_blocks, rows, BS), jnp.bfloat16),
            pltpu.SemaphoreType.DMA((n_blocks,)),
        ],
        compiler_params=pltpu.CompilerParams(vmem_limit_bytes=8 * MIB),
    )(where, virt_density)
    v_across = across(mine)
    far_b = pair(after(far_a, other))
    if aux == 4:
        rest_a = swap(centers, ("groups", "aux"), (groups, aux), lambda g, a: (g, a ^ (2 | g)))
        rest_b = plane(rest_a)
        all_centers = [centers, other, rest_a, rest_b]
    else:
        all_centers = [lax.all_gather(centers, "aux", axis=0)]

    m_parts = [centers, core(centers), far_a, core(far_a), other, core(other), far_b]
    m_parts.append(core(far_b))
    n_early = 3 if aux == 4 else 0
    packed, occ_rows, staged, flag = pl.pallas_call(
        functools.partial(stage, n_early),
        out_shape=[
            jax.ShapeDtypeStruct((basis_total // BS, 2 * BS, KN * BS), jnp.bfloat16),
            jax.ShapeDtypeStruct((rows, basis_total), jnp.bfloat16),
            jax.ShapeDtypeStruct((aux if n_early else 1, KN, rows, BS), jnp.bfloat16),
            jax.ShapeDtypeStruct((8, BS), jnp.float32),
        ],
        in_specs=[scalars] * 2 + [anywhere] * (9 + n_early),
        out_specs=[vmem] * 4,
        scratch_shapes=[
            pltpu.VMEM((8, KN, rows, BS), jnp.bfloat16),
            pltpu.VMEM((basis_total, rows), jnp.bfloat16),
            pltpu.SemaphoreType.DMA((8,)),
            pltpu.SemaphoreType.DMA,
            pltpu.SemaphoreType.DMA((4,)),
        ],
        compiler_params=pltpu.CompilerParams(vmem_limit_bytes=(20 if aux == 4 else 24) * MIB),
    )(where, partner_count, *m_parts, occ_density, *all_centers[:n_early])
    late = all_centers[n_early:]
    moved, flag, *_ = lax.optimization_barrier((v_across, flag, *late))
    v_parts = [mine, core(mine), v_across, core(moved)]
    sums = pl.pallas_call(
        functools.partial(contract, len(all_centers)),
        out_shape=jax.ShapeDtypeStruct((2, aux, BS), jnp.float32),
        in_specs=[scalars] * 3 + [anywhere] * 4 + [vmem] * (3 + len(late)) + [anywhere],
        out_specs=vmem,
        scratch_shapes=[
            pltpu.VMEM((n_blocks, 4, BS, rows), jnp.bfloat16),
            pltpu.VMEM((n_blocks, 2 * BS, basis_total), jnp.bfloat16),
            pltpu.VMEM((2, aux, 8, BS), jnp.float32),
            pltpu.SMEM((n_blocks,), jnp.int32),
            pltpu.SMEM((n_blocks,), jnp.int32),
            pltpu.SemaphoreType.DMA((n_blocks, 4)),
        ],
        compiler_params=pltpu.CompilerParams(vmem_limit_bytes=(20 if aux == 4 else 48) * MIB),
    )(where, partner_list.T, partner_count, *v_parts, packed, occ_rows, staged, *late, flag)

    sums = sums + core(sums)
    diagonal = swap(sums[1], ("aux", "atoms"), (aux, atoms), lambda a, t: (a ^ 1, t ^ 2))
    total = sums[0] + across(sums[0]) + pair(sums[1]) + diagonal
    share = aux // atoms
    row = lax.dynamic_slice_in_dim(total, atom_at * share, share, 0)
    return (row.sum(axis=1) * jnp.float32(-(basis_total ** (-0.5))))[None, :]


def solution(mesh):
    sizes = tuple(mesh.shape[name] for name in ("groups", "aux", "atoms"))
    in_specs = (
        P("atoms", "aux", None, None),
        P(("groups", "atoms"), None),
        P("groups", "atoms"),
        P(),
        P(),
    )
    out_specs = P(("groups", "aux"), "atoms")
    return jax.shard_map(
        functools.partial(on_device, sizes),
        mesh=mesh,
        in_specs=in_specs,
        out_specs=out_specs,
        check_vma=False,
    )
```

```python
import functools

import jax
import jax.numpy as jnp
from jax import lax
from jax.experimental import pallas as pl
from jax.experimental.pallas import tpu as pltpu
from jax.sharding import PartitionSpec as P

BS = 128
KN = 3
MIB = 1 << 20


def swap(x, axes, sizes, move):
    perm = []
    total = 1
    for size in sizes:
        total *= size
    for source in range(total):
        coords, rest = [], source
        for size in reversed(sizes):
            coords.append(rest % size)
            rest //= size
        target = 0
        for size, at in zip(sizes, move(*reversed(coords))):
            target = target * size + at
        perm.append((source, target))
    return lax.ppermute(x, axes, perm)


def select(n_blocks, where, virt_ref, out_ref, buf, sem):
    def copy(i):
        columns = pl.ds(pl.multiple_of((2 * i + where[1]) * BS, BS), BS)
        return pltpu.make_async_copy(virt_ref.at[:, columns], buf.at[i], sem.at[i])

    for i in range(n_blocks):
        copy(i).start()
    for i in range(n_blocks):
        copy(i).wait()
        out_ref[i * BS : (i + 1) * BS, :] = buf[i].T


def after(x, *others):
    return lax.optimization_barrier((x,) + others)[0]


def contract(n_centers, where, plist, pcount, *refs):
    v_refs, m_refs, occ_ref, c_refs = refs[0:4], refs[4:12], refs[12], refs[13 : 13 + n_centers]
    out_ref, prod, acc, listed, place = refs[13 + n_centers :]
    own, parity, plane, aux_at = where[0], where[1], where[2], where[3]
    n_q = acc.shape[1]
    rows = v_refs[0].shape[1]
    blocks_here = rows // BS
    n_places = prod.shape[0]

    def used(b, k):
        block = own * blocks_here + b
        return (k < pcount[block]) & ((plist[k, block] & 1) == parity)

    def column(b, k):
        return plist[k, own * blocks_here + b] >> 1

    for c in range(n_places):
        place[c] = -1
    count = jnp.int32(blocks_here // 2)
    for i in range(blocks_here // 2):
        c = own * (blocks_here // 2) + i
        place[c] = i
        listed[i] = c
    for k in range(1, KN):
        for b in range(blocks_here):
            c = column(b, k)
            new = used(b, k) & (place[c] < 0)

            @pl.when(new)
            def _(c=c, count=count):
                place[c] = count
                listed[count] = c

            count = count + new.astype(jnp.int32)

    @pl.when((count & 1) == 1)
    def _():
        listed[count] = listed[count - 1]

    acc[...] = jnp.zeros_like(acc)

    def one_group(g, carry):
        spans = [pl.ds(pl.multiple_of(listed[2 * g + h] * BS, BS), BS) for h in range(2)]
        for i in range(4):
            for j in range(blocks_here):
                block = (own ^ i) * blocks_here + j
                span = slice(j * BS, (j + 1) * BS)
                parts = [jnp.concatenate([v_refs[i][r, span] for r in spans], axis=0)]
                weights = [jnp.concatenate([m_refs[4 * s + i][0, span, :] for s in range(2)])]
                for k in range(1, KN):
                    p = plist[k, block]
                    shard = (p // blocks_here) ^ own
                    at = pl.ds(pl.multiple_of(lax.rem(p, blocks_here) * BS, BS), BS)
                    part = jnp.concatenate([v_refs[0][r, at] for r in spans], axis=0)
                    for q in range(1, 4):
                        other = jnp.concatenate([v_refs[q][r, at] for r in spans], axis=0)
                        part = jnp.where(shard == q, other, part)
                    parts.append(part)
                    weight = jnp.concatenate([m_refs[4 * s + i][k, span, :] for s in range(2)])
                    weights.append(jnp.where(k < pcount[block], weight, jnp.zeros_like(weight)))
                res = lax.dot_general(
                    jnp.concatenate(parts, axis=1),
                    jnp.concatenate(weights, axis=1),
                    (((1,), (1,)), ((), ())),
                    preferred_element_type=jnp.float32,
                ).astype(jnp.bfloat16)
                at = pl.ds(pl.multiple_of(block * BS, BS), BS)
                for s in range(2):
                    for h in range(2):
                        prod[2 * g + h, s * BS : (s + 1) * BS, at] = res[
                            h * BS : (h + 1) * BS, s * BS : (s + 1) * BS
                        ]
        return carry

    lax.fori_loop(0, (count + 1) >> 1, one_group, 0)

    def tile(at, span, k):
        left = jnp.dot(prod[at], occ_ref[:, span], preferred_element_type=jnp.float32)
        left = left.astype(jnp.bfloat16).astype(jnp.float32)
        left = [left[s * BS : (s + 1) * BS, :].T for s in range(2)]

        def add(q, center):
            center = center.astype(jnp.float32)
            for s in range(2):
                acc[s, q] += (left[s] * center).reshape(BS // 8, 8, BS).sum(axis=0)

        if n_centers == 1:
            lax.fori_loop(0, n_q, lambda q, x: (add(q, c_refs[0][q, k, span, :]), x)[1], 0)
        else:
            for step, c_ref in zip([0, 1, 2 | plane, 3 ^ plane], c_refs):
                add(aux_at ^ step, c_ref[k, span, :])

    for i in range(blocks_here // 2):
        tile(i, pl.ds(pl.multiple_of((2 * i + parity) * BS, BS), BS), 0)
    for k in range(1, KN):
        for b in range(blocks_here):

            @pl.when(used(b, k))
            def _(b=b, k=k):
                tile(place[column(b, k)], slice(b * BS, (b + 1) * BS), k)

    for s in range(2):
        out_ref[s] = acc[s].sum(axis=1)


def on_device(sizes, three_center, virt_density, occ_density, partner_list, partner_count):
    groups, aux, atoms = sizes
    rows = three_center.shape[0]
    basis_total = virt_density.shape[1]
    group_at = lax.axis_index("groups")
    aux_at = lax.axis_index("aux")
    atom_at = lax.axis_index("atoms")
    where = jnp.stack([atom_at, aux_at & 1, group_at, aux_at]).astype(jnp.int32)
    columns = basis_total // 2
    n_blocks = columns // BS

    core = functools.partial(swap, axes=("atoms",), sizes=(atoms,), move=lambda t: (t ^ 1,))
    across = functools.partial(swap, axes=("atoms",), sizes=(atoms,), move=lambda t: (t ^ 2,))
    plane = functools.partial(swap, axes=("groups",), sizes=(groups,), move=lambda g: (g ^ 1,))
    pair = functools.partial(swap, axes=("aux",), sizes=(aux,), move=lambda a: (a ^ 1,))

    anywhere = pl.BlockSpec(memory_space=pltpu.HBM)
    scalars = pl.BlockSpec(memory_space=pltpu.SMEM)
    vmem = pl.BlockSpec(memory_space=pltpu.VMEM)

    centers = three_center[:, 0].transpose(1, 0, 2)
    far_a = across(centers)
    other = pair(centers)
    mine = pl.pallas_call(
        functools.partial(select, n_blocks),
        out_shape=jax.ShapeDtypeStruct((columns, rows), jnp.bfloat16),
        in_specs=[scalars, anywhere],
        out_specs=vmem,
        scratch_shapes=[
            pltpu.VMEM((n_blocks, rows, BS), jnp.bfloat16),
            pltpu.SemaphoreType.DMA((n_blocks,)),
        ],
        compiler_params=pltpu.CompilerParams(vmem_limit_bytes=8 * MIB),
    )(where, virt_density)
    v_across = across(mine)
    if aux == 4:
        rest_a = swap(centers, ("groups", "aux"), (groups, aux), lambda g, a: (g, a ^ (2 | g)))
        rest_b = plane(rest_a)
        all_centers = [centers, other, rest_a, rest_b]
        far_b = pair(after(far_a, other, rest_a))
    else:
        all_centers = [lax.all_gather(centers, "aux", axis=0)]
        far_b = pair(after(far_a, other))

    m_parts = [centers, core(centers), far_a, core(far_a), other, core(other), far_b]
    m_parts.append(core(far_b))
    v_parts = [mine, core(mine), v_across]
    v_parts.append(core(after(v_across, *m_parts[1:], all_centers[-1])))
    sums = pl.pallas_call(
        functools.partial(contract, len(all_centers)),
        out_shape=jax.ShapeDtypeStruct((2, aux, BS), jnp.float32),
        in_specs=[scalars] * 3 + [vmem] * (13 + len(all_centers)),
        out_specs=vmem,
        scratch_shapes=[
            pltpu.VMEM((n_blocks, 2 * BS, basis_total), jnp.bfloat16),
            pltpu.VMEM((2, aux, 8, BS), jnp.float32),
            pltpu.SMEM((n_blocks,), jnp.int32),
            pltpu.SMEM((n_blocks,), jnp.int32),
        ],
        compiler_params=pltpu.CompilerParams(vmem_limit_bytes=(24 if aux == 4 else 48) * MIB),
    )(where, partner_list.T, partner_count, *v_parts, *m_parts, occ_density, *all_centers)

    sums = sums + core(sums)
    diagonal = swap(sums[1], ("aux", "atoms"), (aux, atoms), lambda a, t: (a ^ 1, t ^ 2))
    total = sums[0] + across(sums[0]) + pair(sums[1]) + diagonal
    share = aux // atoms
    row = lax.dynamic_slice_in_dim(total, atom_at * share, share, 0)
    return (row.sum(axis=1) * jnp.float32(-(basis_total ** (-0.5))))[None, :]


def solution(mesh):
    sizes = tuple(mesh.shape[name] for name in ("groups", "aux", "atoms"))
    in_specs = (
        P("atoms", "aux", None, None),
        P(("groups", "atoms"), None),
        P("groups", "atoms"),
        P(),
        P(),
    )
    out_specs = P(("groups", "aux"), "atoms")
    return jax.shard_map(
        functools.partial(on_device, sizes),
        mesh=mesh,
        in_specs=in_specs,
        out_specs=out_specs,
        check_vma=False,
    )
```

```python
import functools

import jax
import jax.numpy as jnp
from jax import lax
from jax.experimental import pallas as pl
from jax.experimental.pallas import tpu as pltpu
from jax.sharding import PartitionSpec as P

BS = 128
KN = 3
MIB = 1 << 20


def swap(x, axes, sizes, move):
    perm = []
    total = 1
    for size in sizes:
        total *= size
    for source in range(total):
        coords, rest = [], source
        for size in reversed(sizes):
            coords.append(rest % size)
            rest //= size
        target = 0
        for size, at in zip(sizes, move(*reversed(coords))):
            target = target * size + at
        perm.append((source, target))
    return lax.ppermute(x, axes, perm)


def select(n_blocks, where, virt_ref, out_ref, buf, sem):
    def copy(i):
        columns = pl.ds(pl.multiple_of((2 * i + where[1]) * BS, BS), BS)
        return pltpu.make_async_copy(virt_ref.at[:, columns], buf.at[i], sem.at[i])

    for i in range(n_blocks):
        copy(i).start()
    for i in range(n_blocks):
        copy(i).wait()
        out_ref[i * BS : (i + 1) * BS, :] = buf[i].T


def after(x, *others):
    return lax.optimization_barrier((x,) + others)[0]


def contract(n_centers, where, plist, pcount, *refs):
    v_refs, m_refs, f_refs, occ_ref = refs[0:4], refs[4:8], refs[8:16], refs[16]
    c_refs = refs[17 : 17 + n_centers]
    out_ref, prod, acc, listed, place = refs[17 + n_centers :]
    own, parity, plane, aux_at = where[0], where[1], where[2], where[3]
    n_q = acc.shape[1]
    rows = v_refs[0].shape[1]
    blocks_here = rows // BS
    n_places = prod.shape[0]

    def used(b, k):
        block = own * blocks_here + b
        return (k < pcount[block]) & ((plist[k, block] & 1) == parity)

    def column(b, k):
        return plist[k, own * blocks_here + b] >> 1

    for c in range(n_places):
        place[c] = -1
    count = jnp.int32(blocks_here // 2)
    for i in range(blocks_here // 2):
        c = own * (blocks_here // 2) + i
        place[c] = i
        listed[i] = c
    for k in range(1, KN):
        for b in range(blocks_here):
            c = column(b, k)
            new = used(b, k) & (place[c] < 0)

            @pl.when(new)
            def _(c=c, count=count):
                place[c] = count
                listed[count] = c

            count = count + new.astype(jnp.int32)

    @pl.when((count & 1) == 1)
    def _():
        listed[count] = listed[count - 1]

    acc[...] = jnp.zeros_like(acc)

    def weight_tile(i, k, j):
        span = slice(j * BS, (j + 1) * BS)
        tiles = []
        for s in range(2):
            if i < 2:
                tiles.append(m_refs[2 * s + i][k, span, :])
            else:
                half, row = divmod(j * BS, rows // 2)
                at = 4 * s + 2 * (i - 2)
                tiles.append(
                    jnp.where(
                        plane == half,
                        f_refs[at][k, row : row + BS, :],
                        f_refs[at + 1][k, row : row + BS, :],
                    )
                )
        return jnp.concatenate(tiles)

    def one_group(g, carry):
        spans = [pl.ds(pl.multiple_of(listed[2 * g + h] * BS, BS), BS) for h in range(2)]
        for i in range(4):
            for j in range(blocks_here):
                block = (own ^ i) * blocks_here + j
                span = slice(j * BS, (j + 1) * BS)
                parts = [jnp.concatenate([v_refs[i][r, span] for r in spans], axis=0)]
                weights = [weight_tile(i, 0, j)]
                for k in range(1, KN):
                    p = plist[k, block]
                    shard = (p // blocks_here) ^ own
                    at = pl.ds(pl.multiple_of(lax.rem(p, blocks_here) * BS, BS), BS)
                    part = jnp.concatenate([v_refs[0][r, at] for r in spans], axis=0)
                    for q in range(1, 4):
                        other = jnp.concatenate([v_refs[q][r, at] for r in spans], axis=0)
                        part = jnp.where(shard == q, other, part)
                    parts.append(part)
                    weight = weight_tile(i, k, j)
                    weights.append(jnp.where(k < pcount[block], weight, jnp.zeros_like(weight)))
                res = lax.dot_general(
                    jnp.concatenate(parts, axis=1),
                    jnp.concatenate(weights, axis=1),
                    (((1,), (1,)), ((), ())),
                    preferred_element_type=jnp.float32,
                ).astype(jnp.bfloat16)
                at = pl.ds(pl.multiple_of(block * BS, BS), BS)
                for s in range(2):
                    for h in range(2):
                        prod[2 * g + h, s * BS : (s + 1) * BS, at] = res[
                            h * BS : (h + 1) * BS, s * BS : (s + 1) * BS
                        ]
        return carry

    lax.fori_loop(0, (count + 1) >> 1, one_group, 0)

    def tile(at, span, k):
        left = jnp.dot(prod[at], occ_ref[:, span], preferred_element_type=jnp.float32)
        left = left.astype(jnp.bfloat16).astype(jnp.float32)
        left = [left[s * BS : (s + 1) * BS, :].T for s in range(2)]

        def add(q, center):
            center = center.astype(jnp.float32)
            for s in range(2):
                acc[s, q] += (left[s] * center).reshape(BS // 8, 8, BS).sum(axis=0)

        if n_centers == 1:
            lax.fori_loop(0, n_q, lambda q, x: (add(q, c_refs[0][q, k, span, :]), x)[1], 0)
        else:
            for step, c_ref in zip([0, 1, 2 | plane, 3 ^ plane], c_refs):
                add(aux_at ^ step, c_ref[k, span, :])

    for i in range(blocks_here // 2):
        tile(i, pl.ds(pl.multiple_of((2 * i + parity) * BS, BS), BS), 0)
    for k in range(1, KN):
        for b in range(blocks_here):

            @pl.when(used(b, k))
            def _(b=b, k=k):
                tile(place[column(b, k)], slice(b * BS, (b + 1) * BS), k)

    for s in range(2):
        out_ref[s] = acc[s].sum(axis=1)


def on_device(sizes, three_center, virt_density, occ_density, partner_list, partner_count):
    groups, aux, atoms = sizes
    rows = three_center.shape[0]
    basis_total = virt_density.shape[1]
    group_at = lax.axis_index("groups")
    aux_at = lax.axis_index("aux")
    atom_at = lax.axis_index("atoms")
    where = jnp.stack([atom_at, aux_at & 1, group_at, aux_at]).astype(jnp.int32)
    columns = basis_total // 2
    n_blocks = columns // BS

    core = functools.partial(swap, axes=("atoms",), sizes=(atoms,), move=lambda t: (t ^ 1,))
    across = functools.partial(swap, axes=("atoms",), sizes=(atoms,), move=lambda t: (t ^ 2,))
    plane = functools.partial(swap, axes=("groups",), sizes=(groups,), move=lambda g: (g ^ 1,))
    pair = functools.partial(swap, axes=("aux",), sizes=(aux,), move=lambda a: (a ^ 1,))

    anywhere = pl.BlockSpec(memory_space=pltpu.HBM)
    scalars = pl.BlockSpec(memory_space=pltpu.SMEM)
    vmem = pl.BlockSpec(memory_space=pltpu.VMEM)

    centers = three_center[:, 0].transpose(1, 0, 2)
    half = rows // 2
    far_half = lax.dynamic_slice_in_dim(centers, group_at * half, half, 1)
    far_x = across(far_half)
    other = pair(centers)
    mine = pl.pallas_call(
        functools.partial(select, n_blocks),
        out_shape=jax.ShapeDtypeStruct((columns, rows), jnp.bfloat16),
        in_specs=[scalars, anywhere],
        out_specs=vmem,
        scratch_shapes=[
            pltpu.VMEM((n_blocks, rows, BS), jnp.bfloat16),
            pltpu.SemaphoreType.DMA((n_blocks,)),
        ],
        compiler_params=pltpu.CompilerParams(vmem_limit_bytes=8 * MIB),
    )(where, after(virt_density, far_half))
    v_across = across(mine)
    far_y = plane(far_x)
    early = [other]
    if aux == 4:
        rest_a = swap(centers, ("groups", "aux"), (groups, aux), lambda g, a: (g, a ^ (2 | g)))
        rest_b = plane(rest_a)
        all_centers = [centers, other, rest_a, rest_b]
        early.append(rest_a)
    else:
        all_centers = [lax.all_gather(centers, "aux", axis=0)]
    pair_x, pair_y = pair(after(far_x, far_y)), pair(far_y)

    far_x_core = core(after(far_x, far_y, *early))
    far_y_core = core(after(far_y, far_x_core))
    centers_core = core(after(centers, far_y_core))
    other_core = core(other)
    m_parts = [centers, centers_core, other, other_core, far_x, far_y, far_x_core, far_y_core]
    m_parts += [pair_x, pair_y, core(pair_x), core(pair_y)]
    v_parts = [mine, core(mine), v_across]
    v_parts.append(core(after(v_across, *m_parts[1:], all_centers[-1])))
    sums = pl.pallas_call(
        functools.partial(contract, len(all_centers)),
        out_shape=jax.ShapeDtypeStruct((2, aux, BS), jnp.float32),
        in_specs=[scalars] * 3 + [vmem] * (17 + len(all_centers)),
        out_specs=vmem,
        scratch_shapes=[
            pltpu.VMEM((n_blocks, 2 * BS, basis_total), jnp.bfloat16),
            pltpu.VMEM((2, aux, 8, BS), jnp.float32),
            pltpu.SMEM((n_blocks,), jnp.int32),
            pltpu.SMEM((n_blocks,), jnp.int32),
        ],
        compiler_params=pltpu.CompilerParams(vmem_limit_bytes=(24 if aux == 4 else 48) * MIB),
    )(where, partner_list.T, partner_count, *v_parts, *m_parts, occ_density, *all_centers)

    sums = sums + core(sums)
    diagonal = swap(sums[1], ("aux", "atoms"), (aux, atoms), lambda a, t: (a ^ 1, t ^ 2))
    total = sums[0] + across(sums[0]) + pair(sums[1]) + diagonal
    share = aux // atoms
    row = lax.dynamic_slice_in_dim(total, atom_at * share, share, 0)
    return (row.sum(axis=1) * jnp.float32(-(basis_total ** (-0.5))))[None, :]


def solution(mesh):
    sizes = tuple(mesh.shape[name] for name in ("groups", "aux", "atoms"))
    in_specs = (
        P("atoms", "aux", None, None),
        P(("groups", "atoms"), None),
        P("groups", "atoms"),
        P(),
        P(),
    )
    out_specs = P(("groups", "aux"), "atoms")
    return jax.shard_map(
        functools.partial(on_device, sizes),
        mesh=mesh,
        in_specs=in_specs,
        out_specs=out_specs,
        check_vma=False,
    )
```

```python
import functools

import jax
import jax.numpy as jnp
from jax import lax
from jax.experimental import pallas as pl
from jax.experimental.pallas import tpu as pltpu
from jax.sharding import PartitionSpec as P

BS = 128
KN = 3
MIB = 1 << 20


def swap(x, axes, sizes, move):
    perm = []
    total = 1
    for size in sizes:
        total *= size
    for source in range(total):
        coords, rest = [], source
        for size in reversed(sizes):
            coords.append(rest % size)
            rest //= size
        target = 0
        for size, at in zip(sizes, move(*reversed(coords))):
            target = target * size + at
        perm.append((source, target))
    return lax.ppermute(x, axes, perm)


def select(n_blocks, where, virt_ref, out_ref, buf, sem):
    def copy(i):
        columns = pl.ds(pl.multiple_of((2 * i + where[1]) * BS, BS), BS)
        return pltpu.make_async_copy(virt_ref.at[:, columns], buf.at[i], sem.at[i])

    for i in range(n_blocks):
        copy(i).start()
    for i in range(n_blocks):
        copy(i).wait()
        out_ref[i * BS : (i + 1) * BS, :] = buf[i].T


def after(x, *others):
    return lax.optimization_barrier((x,) + others)[0]


def contract(n_centers, where, plist, pcount, *refs):
    v_refs, m_refs, f_refs, occ_ref = refs[0:4], refs[4:8], refs[8:16], refs[16]
    c_refs = refs[17 : 17 + n_centers]
    out_ref, prod, acc, listed, place, queue = refs[17 + n_centers :]
    own, parity, plane, aux_at = where[0], where[1], where[2], where[3]
    n_q = acc.shape[1]
    rows = v_refs[0].shape[1]
    blocks_here = rows // BS
    n_places = prod.shape[0]

    def used(b, k):
        block = own * blocks_here + b
        return (k < pcount[block]) & ((plist[k, block] & 1) == parity)

    def column(b, k):
        return plist[k, own * blocks_here + b] >> 1

    for c in range(n_places):
        place[c] = -1
    count = jnp.int32(blocks_here // 2)
    for i in range(blocks_here // 2):
        c = own * (blocks_here // 2) + i
        place[c] = i
        listed[i] = c
    for k in range(1, KN):
        for b in range(blocks_here):
            c = column(b, k)
            new = used(b, k) & (place[c] < 0)

            @pl.when(new)
            def _(c=c, count=count):
                place[c] = count
                listed[count] = c

            count = count + new.astype(jnp.int32)

    @pl.when((count & 1) == 1)
    def _():
        listed[count] = listed[count - 1]

    acc[...] = jnp.zeros_like(acc)

    def weight_tile(i, k, j):
        span = slice(j * BS, (j + 1) * BS)
        tiles = []
        for s in range(2):
            if i < 2:
                tiles.append(m_refs[2 * s + i][k, span, :])
            else:
                half, row = divmod(j * BS, rows // 2)
                at = 4 * s + 2 * (i - 2)
                tiles.append(
                    jnp.where(
                        plane == half,
                        f_refs[at][k, row : row + BS, :],
                        f_refs[at + 1][k, row : row + BS, :],
                    )
                )
        return jnp.concatenate(tiles)

    def one_group(g, carry):
        spans = [pl.ds(pl.multiple_of(listed[2 * g + h] * BS, BS), BS) for h in range(2)]
        for i in range(4):
            for j in range(blocks_here):
                block = (own ^ i) * blocks_here + j
                span = slice(j * BS, (j + 1) * BS)
                parts = [jnp.concatenate([v_refs[i][r, span] for r in spans], axis=0)]
                weights = [weight_tile(i, 0, j)]
                for k in range(1, KN):
                    p = plist[k, block]
                    shard = (p // blocks_here) ^ own
                    at = pl.ds(pl.multiple_of(lax.rem(p, blocks_here) * BS, BS), BS)
                    part = jnp.concatenate([v_refs[0][r, at] for r in spans], axis=0)
                    for q in range(1, 4):
                        other = jnp.concatenate([v_refs[q][r, at] for r in spans], axis=0)
                        part = jnp.where(shard == q, other, part)
                    parts.append(part)
                    weight = weight_tile(i, k, j)
                    weights.append(jnp.where(k < pcount[block], weight, jnp.zeros_like(weight)))
                res = lax.dot_general(
                    jnp.concatenate(parts, axis=1),
                    jnp.concatenate(weights, axis=1),
                    (((1,), (1,)), ((), ())),
                    preferred_element_type=jnp.float32,
                ).astype(jnp.bfloat16)
                at = pl.ds(pl.multiple_of(block * BS, BS), BS)
                for s in range(2):
                    for h in range(2):
                        prod[2 * g + h, s * BS : (s + 1) * BS, at] = res[
                            h * BS : (h + 1) * BS, s * BS : (s + 1) * BS
                        ]
        return carry

    lax.fori_loop(0, (count + 1) >> 1, one_group, 0)

    def tile(at, b, k, weight=None):
        span = pl.ds(pl.multiple_of(b * BS, BS), BS)
        left = jnp.dot(prod[at], occ_ref[:, span], preferred_element_type=jnp.float32)
        left = left.astype(jnp.bfloat16).astype(jnp.float32)
        left = [left[s * BS : (s + 1) * BS, :].T for s in range(2)]
        if weight is not None:
            left = [part * weight for part in left]

        def add(q, center):
            center = center.astype(jnp.float32)
            for s in range(2):
                acc[s, q] += (left[s] * center).reshape(BS // 8, 8, BS).sum(axis=0)

        if n_centers == 1:
            lax.fori_loop(0, n_q, lambda q, x: (add(q, c_refs[0][q, k, span, :]), x)[1], 0)
        else:
            for step, c_ref in zip([0, 1, 2 | plane, 3 ^ plane], c_refs):
                add(aux_at ^ step, c_ref[k, span, :])

    for i in range(blocks_here // 2):
        tile(i, 2 * i + parity, 0)

    tiles = jnp.int32(0)
    for k in range(1, KN):
        for b in range(blocks_here):
            use = used(b, k)

            @pl.when(use)
            def _(b=b, k=k, tiles=tiles):
                queue[tiles] = k * blocks_here + b

            tiles = tiles + use.astype(jnp.int32)

    def two_tiles(i, carry):
        one, two = queue[2 * i], queue[jnp.minimum(2 * i + 1, tiles - 1)]
        weight = (2 * i + 1 < tiles).astype(jnp.float32)
        for code, scale in ((one, None), (two, weight)):
            b, k = code % blocks_here, code // blocks_here
            tile(place[column(b, k)], b, k, scale)
        return carry

    lax.fori_loop(0, (tiles + 1) >> 1, two_tiles, 0)

    for s in range(2):
        out_ref[s] = acc[s].sum(axis=1)


def on_device(sizes, three_center, virt_density, occ_density, partner_list, partner_count):
    groups, aux, atoms = sizes
    rows = three_center.shape[0]
    basis_total = virt_density.shape[1]
    group_at = lax.axis_index("groups")
    aux_at = lax.axis_index("aux")
    atom_at = lax.axis_index("atoms")
    where = jnp.stack([atom_at, aux_at & 1, group_at, aux_at]).astype(jnp.int32)
    columns = basis_total // 2
    n_blocks = columns // BS

    core = functools.partial(swap, axes=("atoms",), sizes=(atoms,), move=lambda t: (t ^ 1,))
    across = functools.partial(swap, axes=("atoms",), sizes=(atoms,), move=lambda t: (t ^ 2,))
    plane = functools.partial(swap, axes=("groups",), sizes=(groups,), move=lambda g: (g ^ 1,))
    pair = functools.partial(swap, axes=("aux",), sizes=(aux,), move=lambda a: (a ^ 1,))

    anywhere = pl.BlockSpec(memory_space=pltpu.HBM)
    scalars = pl.BlockSpec(memory_space=pltpu.SMEM)
    vmem = pl.BlockSpec(memory_space=pltpu.VMEM)

    centers = three_center[:, 0].transpose(1, 0, 2)
    half = rows // 2
    far_half = lax.dynamic_slice_in_dim(centers, group_at * half, half, 1)
    far_x = across(far_half)
    other = pair(centers)
    mine = pl.pallas_call(
        functools.partial(select, n_blocks),
        out_shape=jax.ShapeDtypeStruct((columns, rows), jnp.bfloat16),
        in_specs=[scalars, anywhere],
        out_specs=vmem,
        scratch_shapes=[
            pltpu.VMEM((n_blocks, rows, BS), jnp.bfloat16),
            pltpu.SemaphoreType.DMA((n_blocks,)),
        ],
        compiler_params=pltpu.CompilerParams(vmem_limit_bytes=8 * MIB),
    )(where, after(virt_density, far_half))
    v_across = across(mine)
    far_y = plane(far_x)
    early = [other]
    if aux == 4:
        rest_a = swap(centers, ("groups", "aux"), (groups, aux), lambda g, a: (g, a ^ (2 | g)))
        rest_b = plane(rest_a)
        all_centers = [centers, other, rest_a, rest_b]
        early.append(rest_a)
    else:
        all_centers = [lax.all_gather(centers, "aux", axis=0)]
    pair_x, pair_y = pair(far_x), pair(far_y)

    far_x_core = core(after(far_x, far_y, *early))
    far_y_core = core(after(far_y, far_x_core))
    pair_x_core, pair_y_core = core(pair_x), core(pair_y)
    centers_core = core(after(centers, far_y_core, pair_x_core))
    other_core = core(other)
    m_parts = [centers, centers_core, other, other_core, far_x, far_y, far_x_core, far_y_core]
    m_parts += [pair_x, pair_y, pair_x_core, pair_y_core]
    v_parts = [mine, core(mine), v_across]
    v_parts.append(core(after(v_across, *m_parts[1:], all_centers[-1])))
    sums = pl.pallas_call(
        functools.partial(contract, len(all_centers)),
        out_shape=jax.ShapeDtypeStruct((2, aux, BS), jnp.float32),
        in_specs=[scalars] * 3 + [vmem] * (17 + len(all_centers)),
        out_specs=vmem,
        scratch_shapes=[
            pltpu.VMEM((n_blocks, 2 * BS, basis_total), jnp.bfloat16),
            pltpu.VMEM((2, aux, 8, BS), jnp.float32),
            pltpu.SMEM((n_blocks,), jnp.int32),
            pltpu.SMEM((n_blocks,), jnp.int32),
            pltpu.SMEM((rows // BS * KN,), jnp.int32),
        ],
        compiler_params=pltpu.CompilerParams(vmem_limit_bytes=(24 if aux == 4 else 48) * MIB),
    )(where, partner_list.T, partner_count, *v_parts, *m_parts, occ_density, *all_centers)

    sums = sums + core(sums)
    diagonal = swap(sums[1], ("aux", "atoms"), (aux, atoms), lambda a, t: (a ^ 1, t ^ 2))
    total = sums[0] + across(sums[0]) + pair(sums[1]) + diagonal
    share = aux // atoms
    row = lax.dynamic_slice_in_dim(total, atom_at * share, share, 0)
    return (row.sum(axis=1) * jnp.float32(-(basis_total ** (-0.5))))[None, :]


def solution(mesh):
    sizes = tuple(mesh.shape[name] for name in ("groups", "aux", "atoms"))
    in_specs = (
        P("atoms", "aux", None, None),
        P(("groups", "atoms"), None),
        P("groups", "atoms"),
        P(),
        P(),
    )
    out_specs = P(("groups", "aux"), "atoms")
    return jax.shard_map(
        functools.partial(on_device, sizes),
        mesh=mesh,
        in_specs=in_specs,
        out_specs=out_specs,
        check_vma=False,
    )
```

```python
import functools

import jax
import jax.numpy as jnp
from jax import lax
from jax.experimental import pallas as pl
from jax.experimental.pallas import tpu as pltpu
from jax.sharding import PartitionSpec as P

BS = 128
KN = 3
MIB = 1 << 20


def swap(x, axes, sizes, move):
    perm = []
    total = 1
    for size in sizes:
        total *= size
    for source in range(total):
        coords, rest = [], source
        for size in reversed(sizes):
            coords.append(rest % size)
            rest //= size
        target = 0
        for size, at in zip(sizes, move(*reversed(coords))):
            target = target * size + at
        perm.append((source, target))
    return lax.ppermute(x, axes, perm)


def select(n_blocks, where, virt_ref, out_ref, buf, sem):
    def copy(i):
        columns = pl.ds(pl.multiple_of((2 * i + where[1]) * BS, BS), BS)
        return pltpu.make_async_copy(virt_ref.at[:, columns], buf.at[i], sem.at[i])

    for i in range(n_blocks):
        copy(i).start()
    for i in range(n_blocks):
        copy(i).wait()
        out_ref[i * BS : (i + 1) * BS, :] = buf[i].T


def after(x, *others):
    return lax.optimization_barrier((x,) + others)[0]


def contract(n_centers, where, plist, pcount, *refs):
    v_refs, m_refs, occ_ref, c_refs = refs[0:4], refs[4:12], refs[12], refs[13 : 13 + n_centers]
    out_ref, prod, acc, listed, place = refs[13 + n_centers :]
    own, parity, plane, aux_at = where[0], where[1], where[2], where[3]
    n_q = acc.shape[1]
    rows = v_refs[0].shape[1]
    blocks_here = rows // BS
    n_places = prod.shape[0]

    def used(b, k):
        block = own * blocks_here + b
        return (k < pcount[block]) & ((plist[k, block] & 1) == parity)

    def column(b, k):
        return plist[k, own * blocks_here + b] >> 1

    for c in range(n_places):
        place[c] = -1
    count = jnp.int32(blocks_here // 2)
    for i in range(blocks_here // 2):
        c = own * (blocks_here // 2) + i
        place[c] = i
        listed[i] = c
    for k in range(1, KN):
        for b in range(blocks_here):
            c = column(b, k)
            new = used(b, k) & (place[c] < 0)

            @pl.when(new)
            def _(c=c, count=count):
                place[c] = count
                listed[count] = c

            count = count + new.astype(jnp.int32)

    @pl.when((count & 1) == 1)
    def _():
        listed[count] = listed[count - 1]

    acc[...] = jnp.zeros_like(acc)

    def one_group(g, carry):
        spans = [pl.ds(pl.multiple_of(listed[2 * g + h] * BS, BS), BS) for h in range(2)]
        for i in range(4):
            for j in range(blocks_here):
                block = (own ^ i) * blocks_here + j
                span = slice(j * BS, (j + 1) * BS)
                parts = [jnp.concatenate([v_refs[i][r, span] for r in spans], axis=0)]
                weights = [jnp.concatenate([m_refs[4 * s + i][0, span, :] for s in range(2)])]
                for k in range(1, KN):
                    p = plist[k, block]
                    shard = (p // blocks_here) ^ own
                    at = pl.ds(pl.multiple_of(lax.rem(p, blocks_here) * BS, BS), BS)
                    part = jnp.concatenate([v_refs[0][r, at] for r in spans], axis=0)
                    for q in range(1, 4):
                        other = jnp.concatenate([v_refs[q][r, at] for r in spans], axis=0)
                        part = jnp.where(shard == q, other, part)
                    parts.append(part)
                    weight = jnp.concatenate([m_refs[4 * s + i][k, span, :] for s in range(2)])
                    weights.append(jnp.where(k < pcount[block], weight, jnp.zeros_like(weight)))
                res = lax.dot_general(
                    jnp.concatenate(parts, axis=1),
                    jnp.concatenate(weights, axis=1),
                    (((1,), (1,)), ((), ())),
                    preferred_element_type=jnp.float32,
                ).astype(jnp.bfloat16)
                at = pl.ds(pl.multiple_of(block * BS, BS), BS)
                for s in range(2):
                    for h in range(2):
                        prod[2 * g + h, s * BS : (s + 1) * BS, at] = res[
                            h * BS : (h + 1) * BS, s * BS : (s + 1) * BS
                        ]
        return carry

    lax.fori_loop(0, (count + 1) >> 1, one_group, 0)

    def tile(at, span, k):
        left = jnp.dot(prod[at], occ_ref[:, span], preferred_element_type=jnp.float32)
        left = left.astype(jnp.bfloat16).astype(jnp.float32)
        left = [left[s * BS : (s + 1) * BS, :].T for s in range(2)]

        def add(q, center):
            center = center.astype(jnp.float32)
            for s in range(2):
                acc[s, q] += (left[s] * center).reshape(BS // 8, 8, BS).sum(axis=0)

        if n_centers == 1:
            lax.fori_loop(0, n_q, lambda q, x: (add(q, c_refs[0][q, k, span, :]), x)[1], 0)
        else:
            for step, c_ref in zip([0, 1, 2 | plane, 3 ^ plane], c_refs):
                add(aux_at ^ step, c_ref[k, span, :])

    for i in range(blocks_here // 2):
        tile(i, pl.ds(pl.multiple_of((2 * i + parity) * BS, BS), BS), 0)
    for k in range(1, KN):
        for b in range(blocks_here):

            @pl.when(used(b, k))
            def _(b=b, k=k):
                tile(place[column(b, k)], slice(b * BS, (b + 1) * BS), k)

    for s in range(2):
        out_ref[s] = acc[s].sum(axis=1)


def on_device(sizes, three_center, virt_density, occ_density, partner_list, partner_count):
    groups, aux, atoms = sizes
    rows = three_center.shape[0]
    basis_total = virt_density.shape[1]
    group_at = lax.axis_index("groups")
    aux_at = lax.axis_index("aux")
    atom_at = lax.axis_index("atoms")
    where = jnp.stack([atom_at, aux_at & 1, group_at, aux_at]).astype(jnp.int32)
    columns = basis_total // 2
    n_blocks = columns // BS

    core = functools.partial(swap, axes=("atoms",), sizes=(atoms,), move=lambda t: (t ^ 1,))
    across = functools.partial(swap, axes=("atoms",), sizes=(atoms,), move=lambda t: (t ^ 2,))
    plane = functools.partial(swap, axes=("groups",), sizes=(groups,), move=lambda g: (g ^ 1,))
    pair = functools.partial(swap, axes=("aux",), sizes=(aux,), move=lambda a: (a ^ 1,))

    anywhere = pl.BlockSpec(memory_space=pltpu.HBM)
    scalars = pl.BlockSpec(memory_space=pltpu.SMEM)
    vmem = pl.BlockSpec(memory_space=pltpu.VMEM)

    centers = three_center[:, 0].transpose(1, 0, 2)
    far_a = across(centers)
    other = pair(centers)
    mine = pl.pallas_call(
        functools.partial(select, n_blocks),
        out_shape=jax.ShapeDtypeStruct((columns, rows), jnp.bfloat16),
        in_specs=[scalars, anywhere],
        out_specs=vmem,
        scratch_shapes=[
            pltpu.VMEM((n_blocks, rows, BS), jnp.bfloat16),
            pltpu.SemaphoreType.DMA((n_blocks,)),
        ],
        compiler_params=pltpu.CompilerParams(vmem_limit_bytes=8 * MIB),
    )(where, virt_density)
    v_across = across(mine)
    counts = core(after(partner_count, far_a))
    if aux == 4:
        rest_a = swap(centers, ("groups", "aux"), (groups, aux), lambda g, a: (g, a ^ (2 | g)))
        rest_b = plane(rest_a)
        all_centers = [centers, other, rest_a, rest_b]
        far_b = pair(after(far_a, other, rest_a, counts))
    else:
        all_centers = [lax.all_gather(centers, "aux", axis=0)]
        far_b = pair(after(far_a, other))

    m_parts = [centers, core(centers), far_a, core(far_a), other, core(other), far_b]
    m_parts.append(core(far_b))
    v_parts = [mine, core(mine), v_across]
    v_parts.append(core(after(v_across, *m_parts[1:], all_centers[-1])))
    sums = pl.pallas_call(
        functools.partial(contract, len(all_centers)),
        out_shape=jax.ShapeDtypeStruct((2, aux, BS), jnp.float32),
        in_specs=[scalars] * 3 + [vmem] * (13 + len(all_centers)),
        out_specs=vmem,
        scratch_shapes=[
            pltpu.VMEM((n_blocks, 2 * BS, basis_total), jnp.bfloat16),
            pltpu.VMEM((2, aux, 8, BS), jnp.float32),
            pltpu.SMEM((n_blocks,), jnp.int32),
            pltpu.SMEM((n_blocks,), jnp.int32),
        ],
        compiler_params=pltpu.CompilerParams(vmem_limit_bytes=(24 if aux == 4 else 48) * MIB),
    )(where, partner_list.T, counts, *v_parts, *m_parts, occ_density, *all_centers)

    sums = sums + core(sums)
    diagonal = swap(sums[1], ("aux", "atoms"), (aux, atoms), lambda a, t: (a ^ 1, t ^ 2))
    total = sums[0] + across(sums[0]) + pair(sums[1]) + diagonal
    share = aux // atoms
    row = lax.dynamic_slice_in_dim(total, atom_at * share, share, 0)
    return (row.sum(axis=1) * jnp.float32(-(basis_total ** (-0.5))))[None, :]


def solution(mesh):
    sizes = tuple(mesh.shape[name] for name in ("groups", "aux", "atoms"))
    in_specs = (
        P("atoms", "aux", None, None),
        P(("groups", "atoms"), None),
        P("groups", "atoms"),
        P(),
        P(),
    )
    out_specs = P(("groups", "aux"), "atoms")
    return jax.shard_map(
        functools.partial(on_device, sizes),
        mesh=mesh,
        in_specs=in_specs,
        out_specs=out_specs,
        check_vma=False,
    )
```

```python
import functools

import jax
import jax.numpy as jnp
from jax import lax
from jax.experimental import pallas as pl
from jax.experimental.pallas import tpu as pltpu
from jax.sharding import PartitionSpec as P

BS = 128
KN = 3
MIB = 1 << 20


def swap(x, axes, sizes, move):
    perm = []
    total = 1
    for size in sizes:
        total *= size
    for source in range(total):
        coords, rest = [], source
        for size in reversed(sizes):
            coords.append(rest % size)
            rest //= size
        target = 0
        for size, at in zip(sizes, move(*reversed(coords))):
            target = target * size + at
        perm.append((source, target))
    return lax.ppermute(x, axes, perm)


def select(n_blocks, where, virt_ref, out_ref, buf, sem):
    def copy(i):
        columns = pl.ds(pl.multiple_of((2 * i + where[1]) * BS, BS), BS)
        return pltpu.make_async_copy(virt_ref.at[:, columns], buf.at[i], sem.at[i])

    for i in range(n_blocks):
        copy(i).start()
    for i in range(n_blocks):
        copy(i).wait()
        out_ref[i * BS : (i + 1) * BS, :] = buf[i].T


def after(x, *others):
    return lax.optimization_barrier((x,) + others)[0]


def contract(n_centers, where, plist, pcount, *refs):
    v_refs, m_refs, occ_ref, c_refs = refs[0:4], refs[4:12], refs[12], refs[13 : 13 + n_centers]
    out_ref, prod, acc, listed, place = refs[13 + n_centers :]
    own, parity, plane, aux_at = where[0], where[1], where[2], where[3]
    n_q = acc.shape[1]
    rows = v_refs[0].shape[1]
    blocks_here = rows // BS
    n_places = prod.shape[0]

    def used(b, k):
        block = own * blocks_here + b
        return (k < pcount[block]) & ((plist[k, block] & 1) == parity)

    def column(b, k):
        return plist[k, own * blocks_here + b] >> 1

    for c in range(n_places):
        place[c] = -1
    count = jnp.int32(blocks_here // 2)
    for i in range(blocks_here // 2):
        c = own * (blocks_here // 2) + i
        place[c] = i
        listed[i] = c
    for k in range(1, KN):
        for b in range(blocks_here):
            c = column(b, k)
            new = used(b, k) & (place[c] < 0)

            @pl.when(new)
            def _(c=c, count=count):
                place[c] = count
                listed[count] = c

            count = count + new.astype(jnp.int32)

    @pl.when((count & 1) == 1)
    def _():
        listed[count] = listed[count - 1]

    acc[...] = jnp.zeros_like(acc)

    def one_group(g, carry):
        spans = [pl.ds(pl.multiple_of(listed[2 * g + h] * BS, BS), BS) for h in range(2)]
        for i in range(4):
            for j in range(blocks_here):
                block = (own ^ i) * blocks_here + j
                span = slice(j * BS, (j + 1) * BS)
                parts = [jnp.concatenate([v_refs[i][r, span] for r in spans], axis=0)]
                weights = [jnp.concatenate([m_refs[4 * s + i][0, span, :] for s in range(2)])]
                for k in range(1, KN):
                    p = plist[k, block]
                    shard = (p // blocks_here) ^ own
                    at = pl.ds(pl.multiple_of(lax.rem(p, blocks_here) * BS, BS), BS)
                    part = jnp.concatenate([v_refs[0][r, at] for r in spans], axis=0)
                    for q in range(1, 4):
                        other = jnp.concatenate([v_refs[q][r, at] for r in spans], axis=0)
                        part = jnp.where(shard == q, other, part)
                    parts.append(part)
                    weight = jnp.concatenate([m_refs[4 * s + i][k, span, :] for s in range(2)])
                    weights.append(jnp.where(k < pcount[block], weight, jnp.zeros_like(weight)))
                res = lax.dot_general(
                    jnp.concatenate(parts, axis=1),
                    jnp.concatenate(weights, axis=1),
                    (((1,), (1,)), ((), ())),
                    preferred_element_type=jnp.float32,
                ).astype(jnp.bfloat16)
                at = pl.ds(pl.multiple_of(block * BS, BS), BS)
                for s in range(2):
                    for h in range(2):
                        prod[2 * g + h, s * BS : (s + 1) * BS, at] = res[
                            h * BS : (h + 1) * BS, s * BS : (s + 1) * BS
                        ]
        return carry

    lax.fori_loop(0, (count + 1) >> 1, one_group, 0)

    def tile(at, span, k):
        left = jnp.dot(prod[at], occ_ref[:, span], preferred_element_type=jnp.float32)
        left = left.astype(jnp.bfloat16).astype(jnp.float32)
        left = [left[s * BS : (s + 1) * BS, :].T for s in range(2)]

        def add(q, center):
            center = center.astype(jnp.float32)
            for s in range(2):
                acc[s, q] += (left[s] * center).reshape(BS // 8, 8, BS).sum(axis=0)

        if n_centers == 1:
            lax.fori_loop(0, n_q, lambda q, x: (add(q, c_refs[0][q, k, span, :]), x)[1], 0)
        else:
            for step, c_ref in zip([0, 1, 2 | plane, 3 ^ plane], c_refs):
                add(aux_at ^ step, c_ref[k, span, :])

    for i in range(blocks_here // 2):
        tile(i, pl.ds(pl.multiple_of((2 * i + parity) * BS, BS), BS), 0)
    for k in range(1, KN):
        for b in range(blocks_here):

            @pl.when(used(b, k))
            def _(b=b, k=k):
                tile(place[column(b, k)], slice(b * BS, (b + 1) * BS), k)

    for s in range(2):
        out_ref[s] = acc[s].sum(axis=1)


def on_device(sizes, three_center, virt_density, occ_density, partner_list, partner_count):
    groups, aux, atoms = sizes
    rows = three_center.shape[0]
    basis_total = virt_density.shape[1]
    group_at = lax.axis_index("groups")
    aux_at = lax.axis_index("aux")
    atom_at = lax.axis_index("atoms")
    where = jnp.stack([atom_at, aux_at & 1, group_at, aux_at]).astype(jnp.int32)
    columns = basis_total // 2
    n_blocks = columns // BS

    core = functools.partial(swap, axes=("atoms",), sizes=(atoms,), move=lambda t: (t ^ 1,))
    across = functools.partial(swap, axes=("atoms",), sizes=(atoms,), move=lambda t: (t ^ 2,))
    plane = functools.partial(swap, axes=("groups",), sizes=(groups,), move=lambda g: (g ^ 1,))
    pair = functools.partial(swap, axes=("aux",), sizes=(aux,), move=lambda a: (a ^ 1,))

    anywhere = pl.BlockSpec(memory_space=pltpu.HBM)
    scalars = pl.BlockSpec(memory_space=pltpu.SMEM)
    vmem = pl.BlockSpec(memory_space=pltpu.VMEM)

    centers = three_center[:, 0].transpose(1, 0, 2)
    far_a = across(centers)
    other = pair(centers)
    mine = pl.pallas_call(
        functools.partial(select, n_blocks),
        out_shape=jax.ShapeDtypeStruct((columns, rows), jnp.bfloat16),
        in_specs=[scalars, anywhere],
        out_specs=vmem,
        scratch_shapes=[
            pltpu.VMEM((n_blocks, rows, BS), jnp.bfloat16),
            pltpu.SemaphoreType.DMA((n_blocks,)),
        ],
        compiler_params=pltpu.CompilerParams(vmem_limit_bytes=8 * MIB),
    )(where, virt_density)
    v_across = across(mine)
    counts = core(after(partner_count, far_a))
    if aux == 4:
        rest_a = swap(centers, ("groups", "aux"), (groups, aux), lambda g, a: (g, a ^ (2 | g)))
        rest_b = plane(rest_a)
        all_centers = [centers, other, rest_a, rest_b]
        far_b = pair(after(far_a, other, rest_a, counts))
    else:
        all_centers = [lax.all_gather(centers, "aux", axis=0)]
        far_b = pair(after(far_a, other))

    m_parts = [centers, core(centers), far_a, core(far_a), other, core(other), far_b]
    m_parts.append(core(far_b))
    mine_core = core(mine)
    moved = core(after(v_across, *m_parts[1:], all_centers[-1], mine_core))
    v_parts = [mine, mine_core, v_across, moved]
    sums = pl.pallas_call(
        functools.partial(contract, len(all_centers)),
        out_shape=jax.ShapeDtypeStruct((2, aux, BS), jnp.float32),
        in_specs=[scalars] * 3 + [vmem] * (13 + len(all_centers)),
        out_specs=vmem,
        scratch_shapes=[
            pltpu.VMEM((n_blocks, 2 * BS, basis_total), jnp.bfloat16),
            pltpu.VMEM((2, aux, 8, BS), jnp.float32),
            pltpu.SMEM((n_blocks,), jnp.int32),
            pltpu.SMEM((n_blocks,), jnp.int32),
        ],
        compiler_params=pltpu.CompilerParams(vmem_limit_bytes=(24 if aux == 4 else 48) * MIB),
    )(where, partner_list.T, counts, *v_parts, *m_parts, occ_density, *all_centers)

    sums = sums + core(sums)
    diagonal = swap(sums[1], ("aux", "atoms"), (aux, atoms), lambda a, t: (a ^ 1, t ^ 2))
    total = sums[0] + across(sums[0]) + pair(sums[1]) + diagonal
    share = aux // atoms
    row = lax.dynamic_slice_in_dim(total, atom_at * share, share, 0)
    return (row.sum(axis=1) * jnp.float32(-(basis_total ** (-0.5))))[None, :]


def solution(mesh):
    sizes = tuple(mesh.shape[name] for name in ("groups", "aux", "atoms"))
    in_specs = (
        P("atoms", "aux", None, None),
        P(("groups", "atoms"), None),
        P("groups", "atoms"),
        P(),
        P(),
    )
    out_specs = P(("groups", "aux"), "atoms")
    return jax.shard_map(
        functools.partial(on_device, sizes),
        mesh=mesh,
        in_specs=in_specs,
        out_specs=out_specs,
        check_vma=False,
    )
```

```python
import functools

import jax
import jax.numpy as jnp
from jax import lax
from jax.experimental import pallas as pl
from jax.experimental.pallas import tpu as pltpu
from jax.sharding import PartitionSpec as P

BS = 128
KN = 3
MIB = 1 << 20


def swap(x, axes, sizes, move):
    perm = []
    total = 1
    for size in sizes:
        total *= size
    for source in range(total):
        coords, rest = [], source
        for size in reversed(sizes):
            coords.append(rest % size)
            rest //= size
        target = 0
        for size, at in zip(sizes, move(*reversed(coords))):
            target = target * size + at
        perm.append((source, target))
    return lax.ppermute(x, axes, perm)


def select(n_blocks, where, virt_ref, out_ref, buf, sem):
    def copy(i):
        columns = pl.ds(pl.multiple_of((2 * i + where[1]) * BS, BS), BS)
        return pltpu.make_async_copy(virt_ref.at[:, columns], buf.at[i], sem.at[i])

    for i in range(n_blocks):
        copy(i).start()
    for i in range(n_blocks):
        copy(i).wait()
        out_ref[i * BS : (i + 1) * BS, :] = buf[i].T


def after(x, *others):
    return lax.optimization_barrier((x,) + others)[0]


def contract(n_centers, where, plist, pcount, *refs):
    v_refs, m_refs, occ_ref, c_refs = refs[0:4], refs[4:12], refs[12], refs[13 : 13 + n_centers]
    out_ref, prod, acc, listed, place = refs[13 + n_centers :]
    own, parity, plane, aux_at = where[0], where[1], where[2], where[3]
    n_q = acc.shape[1]
    rows = v_refs[0].shape[1]
    blocks_here = rows // BS
    n_places = prod.shape[0]

    def used(b, k):
        block = own * blocks_here + b
        return (k < pcount[block]) & ((plist[k, block] & 1) == parity)

    def column(b, k):
        return plist[k, own * blocks_here + b] >> 1

    for c in range(n_places):
        place[c] = -1
    count = jnp.int32(blocks_here // 2)
    for i in range(blocks_here // 2):
        c = own * (blocks_here // 2) + i
        place[c] = i
        listed[i] = c
    for k in range(1, KN):
        for b in range(blocks_here):
            c = column(b, k)
            new = used(b, k) & (place[c] < 0)

            @pl.when(new)
            def _(c=c, count=count):
                place[c] = count
                listed[count] = c

            count = count + new.astype(jnp.int32)

    @pl.when((count & 1) == 1)
    def _():
        listed[count] = listed[count - 1]

    acc[...] = jnp.zeros_like(acc)

    def one_group(g, carry):
        spans = [pl.ds(pl.multiple_of(listed[2 * g + h] * BS, BS), BS) for h in range(2)]
        for i in range(4):
            for j in range(blocks_here):
                block = (own ^ i) * blocks_here + j
                span = slice(j * BS, (j + 1) * BS)
                parts = [jnp.concatenate([v_refs[i][r, span] for r in spans], axis=0)]
                weights = [jnp.concatenate([m_refs[4 * s + i][0, span, :] for s in range(2)])]
                for k in range(1, KN):
                    p = plist[k, block]
                    shard = (p // blocks_here) ^ own
                    at = pl.ds(pl.multiple_of(lax.rem(p, blocks_here) * BS, BS), BS)
                    part = jnp.concatenate([v_refs[0][r, at] for r in spans], axis=0)
                    for q in range(1, 4):
                        other = jnp.concatenate([v_refs[q][r, at] for r in spans], axis=0)
                        part = jnp.where(shard == q, other, part)
                    parts.append(part)
                    weight = jnp.concatenate([m_refs[4 * s + i][k, span, :] for s in range(2)])
                    weights.append(jnp.where(k < pcount[block], weight, jnp.zeros_like(weight)))
                res = lax.dot_general(
                    jnp.concatenate(parts, axis=1),
                    jnp.concatenate(weights, axis=1),
                    (((1,), (1,)), ((), ())),
                    preferred_element_type=jnp.float32,
                ).astype(jnp.bfloat16)
                at = pl.ds(pl.multiple_of(block * BS, BS), BS)
                for s in range(2):
                    for h in range(2):
                        prod[2 * g + h, s * BS : (s + 1) * BS, at] = res[
                            h * BS : (h + 1) * BS, s * BS : (s + 1) * BS
                        ]
        return carry

    lax.fori_loop(0, (count + 1) >> 1, one_group, 0)

    def tile(at, span, k):
        left = jnp.dot(prod[at], occ_ref[:, span], preferred_element_type=jnp.float32)
        left = left.astype(jnp.bfloat16).astype(jnp.float32)
        left = [left[s * BS : (s + 1) * BS, :].T for s in range(2)]

        def add(q, center):
            center = center.astype(jnp.float32)
            for s in range(2):
                acc[s, q] += (left[s] * center).reshape(BS // 8, 8, BS).sum(axis=0)

        if n_centers == 1:
            lax.fori_loop(0, n_q, lambda q, x: (add(q, c_refs[0][q, k, span, :]), x)[1], 0)
        else:
            for step, c_ref in zip([0, 1, 2 | plane, 3 ^ plane], c_refs):
                add(aux_at ^ step, c_ref[k, span, :])

    for i in range(blocks_here // 2):
        tile(i, pl.ds(pl.multiple_of((2 * i + parity) * BS, BS), BS), 0)
    for k in range(1, KN):
        for b in range(blocks_here):

            @pl.when(used(b, k))
            def _(b=b, k=k):
                tile(place[column(b, k)], slice(b * BS, (b + 1) * BS), k)

    for s in range(2):
        out_ref[s] = acc[s].sum(axis=1)


def on_device(sizes, three_center, virt_density, occ_density, partner_list, partner_count):
    groups, aux, atoms = sizes
    rows = three_center.shape[0]
    basis_total = virt_density.shape[1]
    group_at = lax.axis_index("groups")
    aux_at = lax.axis_index("aux")
    atom_at = lax.axis_index("atoms")
    where = jnp.stack([atom_at, aux_at & 1, group_at, aux_at]).astype(jnp.int32)
    columns = basis_total // 2
    n_blocks = columns // BS

    core = functools.partial(swap, axes=("atoms",), sizes=(atoms,), move=lambda t: (t ^ 1,))
    across = functools.partial(swap, axes=("atoms",), sizes=(atoms,), move=lambda t: (t ^ 2,))
    plane = functools.partial(swap, axes=("groups",), sizes=(groups,), move=lambda g: (g ^ 1,))
    pair = functools.partial(swap, axes=("aux",), sizes=(aux,), move=lambda a: (a ^ 1,))

    anywhere = pl.BlockSpec(memory_space=pltpu.HBM)
    scalars = pl.BlockSpec(memory_space=pltpu.SMEM)
    vmem = pl.BlockSpec(memory_space=pltpu.VMEM)

    centers = three_center[:, 0].transpose(1, 0, 2)
    far_a = across(centers)
    other = pair(centers)
    mine = pl.pallas_call(
        functools.partial(select, n_blocks),
        out_shape=jax.ShapeDtypeStruct((columns, rows), jnp.bfloat16),
        in_specs=[scalars, anywhere],
        out_specs=vmem,
        scratch_shapes=[
            pltpu.VMEM((n_blocks, rows, BS), jnp.bfloat16),
            pltpu.SemaphoreType.DMA((n_blocks,)),
        ],
        compiler_params=pltpu.CompilerParams(vmem_limit_bytes=8 * MIB),
    )(where, virt_density)
    v_across = across(mine)
    counts = core(after(partner_count, far_a))
    if aux == 4:
        rest_a = swap(centers, ("groups", "aux"), (groups, aux), lambda g, a: (g, a ^ (2 | g)))
        rest_b = plane(after(rest_a, counts))
        all_centers = [centers, other, rest_a, rest_b]
        far_b = pair(after(far_a, other, rest_a, counts))
    else:
        all_centers = [lax.all_gather(centers, "aux", axis=0)]
        far_b = pair(after(far_a, other))

    m_parts = [centers, core(centers), far_a, core(far_a), other, core(other), far_b]
    m_parts.append(core(far_b))
    mine_core = core(mine)
    moved = core(after(v_across, *m_parts[1:], all_centers[-1], mine_core))
    v_parts = [mine, mine_core, v_across, moved]
    sums = pl.pallas_call(
        functools.partial(contract, len(all_centers)),
        out_shape=jax.ShapeDtypeStruct((2, aux, BS), jnp.float32),
        in_specs=[scalars] * 3 + [vmem] * (13 + len(all_centers)),
        out_specs=vmem,
        scratch_shapes=[
            pltpu.VMEM((n_blocks, 2 * BS, basis_total), jnp.bfloat16),
            pltpu.VMEM((2, aux, 8, BS), jnp.float32),
            pltpu.SMEM((n_blocks,), jnp.int32),
            pltpu.SMEM((n_blocks,), jnp.int32),
        ],
        compiler_params=pltpu.CompilerParams(vmem_limit_bytes=(24 if aux == 4 else 48) * MIB),
    )(where, partner_list.T, counts, *v_parts, *m_parts, occ_density, *all_centers)

    sums = sums + core(sums)
    diagonal = swap(sums[1], ("aux", "atoms"), (aux, atoms), lambda a, t: (a ^ 1, t ^ 2))
    total = sums[0] + across(sums[0]) + pair(sums[1]) + diagonal
    share = aux // atoms
    row = lax.dynamic_slice_in_dim(total, atom_at * share, share, 0)
    return (row.sum(axis=1) * jnp.float32(-(basis_total ** (-0.5))))[None, :]


def solution(mesh):
    sizes = tuple(mesh.shape[name] for name in ("groups", "aux", "atoms"))
    in_specs = (
        P("atoms", "aux", None, None),
        P(("groups", "atoms"), None),
        P("groups", "atoms"),
        P(),
        P(),
    )
    out_specs = P(("groups", "aux"), "atoms")
    return jax.shard_map(
        functools.partial(on_device, sizes),
        mesh=mesh,
        in_specs=in_specs,
        out_specs=out_specs,
        check_vma=False,
    )
```
